256 devices in a mesh: dap: 64 (over z_lo, y, x, core), grp: 4 (over z_hi).
Axes of the slice: x: 4, y: 4, z: 8 (z_hi: 4, z_lo: 2; z = z_hi * 2 + z_lo), core: 2. Of those that a mesh axis runs over, the one named last changes fastest.
Arguments:
- pair_map: bfloat16 [512, 512, 128], P(('dap', 'grp')), may hold values from -6 to 6
- pair_mask: int32 [512, 512], P(('dap', 'grp')), may hold values 0 or 1
- edge_weights: bfloat16 [2, 128, 512], replicated, may hold values from -0.5 to 0.5
- gate_weights: bfloat16 [2, 128, 128], replicated, may hold values from -0.5 to 0.5
- out_weights: bfloat16 [2, 128, 128], replicated, may hold values from -0.5 to 0.5
- norm_gains: float32 [2, 2, 128], replicated, may hold values from 0.1 to 1.9
Outputs:
- updated: bfloat16 [512, 512, 128], P(('dap', 'grp'))
The draws below stay inside these ranges and needn't reach their ends.
All inputs are finite; a program needn't handle non-finite values. No bound on the sum of `pair_mask` on one device may be relied on, other than what follows from the above.
Results may differ from the reference program's by a relative error of at most 0.018.
Values may be sent and summed in bfloat16 or wider, within the bound.
A program may use at most 64 MiB of HBM per device.

```python
import jax
import jax.numpy as jnp
from jax import lax

C = 128
H = 128
N = 512


def set_ends(result, key, low, largest):
    place = [jax.random.randint(jax.random.fold_in(key, axis), (), 0, length) for axis, length in enumerate(result.shape)]
    widest = result.shape.index(max(result.shape))
    beside = place[:widest] + [(place[widest] + 1) % result.shape[widest]] + place[widest + 1:]
    return result.at[tuple(place)].set(low).at[tuple(beside)].set(largest)


def steps_of(key, shape, split, least, high):
    def one(axis_at, parts):
        heights = jax.random.uniform(jax.random.fold_in(jax.random.fold_in(key, 6), axis_at), (parts,), jnp.float32, least / len(split), high / len(split))
        return jnp.repeat(jnp.exp(heights), shape[axis_at] // parts).reshape((-1,) + (1,) * (len(shape) - axis_at - 1))

    factor_of = one(*split[0])
    for cut in split[1:]:
        factor_of = factor_of * one(*cut)
    return factor_of


def noise(key, dims, spread, most, pieces=(), kind=jnp.bfloat16):
    gain = steps_of(key, dims, pieces, -0.22, 0.18) if pieces else 1.0
    drawn = jax.random.normal(key, dims, jnp.float32) * spread * gain
    return jnp.minimum(jnp.maximum(drawn, -most), most).astype(kind)


def setup_inputs(seed: int = 0) -> dict:
    keys = jax.random.split(jax.random.key(seed), 7)
    return {
        "pair_map": noise(keys[0], (N, N, C), 1.0, 6.0, ((0, 256),)),
        "pair_mask": set_ends((jax.random.randint(keys[1], (N, N), 0, 8) < 7).astype(jnp.int32), jax.random.fold_in(keys[1], 1), 0, 1),
        "edge_weights": noise(keys[2], (2, C, 4 * H), C ** -0.5, 0.5),
        "gate_weights": noise(keys[3], (2, C, C), C ** -0.5, 0.5),
        "out_weights": noise(keys[4], (2, H, C), H ** -0.5, 0.5),
        "norm_gains": jnp.clip(1.0 + 0.18 * jax.random.normal(keys[5], (2, 2, C), jnp.float32), 0.1, 1.9),
    }


def normalize(values, axis):
    average = lax.optimization_barrier(jnp.mean(values, axis=axis, keepdims=True))
    centred = values - average
    variance = lax.optimization_barrier(jnp.mean(centred * centred, axis=axis, keepdims=True))
    return centred * lax.rsqrt(variance + 1e-05)

def edge_maps(current, pair_mask, weights, norm_gain):

    def one_row(row_items):
        pair_row, mask_row = row_items
        normed = (normalize(pair_row.astype(jnp.float32), -1) * norm_gain).astype(jnp.bfloat16)
        projected = jnp.dot(normed, weights, preferred_element_type=jnp.float32)
        mask_col = mask_row.astype(jnp.float32)[:, None]
        left_edges = (jax.nn.sigmoid(projected[:, :H]) * projected[:, H:2 * H] * mask_col).astype(jnp.bfloat16)
        right_edges = (jax.nn.sigmoid(projected[:, 2 * H:3 * H]) * projected[:, 3 * H:] * mask_col).astype(jnp.bfloat16)
        return (normed, left_edges.T, right_edges.T)
    normed, left_edges, right_edges = lax.map(one_row, (current, pair_mask))
    return (normed, jnp.transpose(left_edges, (1, 0, 2)), jnp.transpose(right_edges, (1, 0, 2)))

def finish(current, normed, product_map, norm_gain, out_weight, gate_weight):
    by_rows = jnp.transpose(product_map, (1, 0, 2))

    def one_row(row_items):
        product_row, pair_row, normed_row = row_items
        scaled = (normalize(product_row.astype(jnp.float32), 0) * norm_gain[:, None]).astype(jnp.bfloat16)
        projected = jnp.dot(scaled.T, out_weight, preferred_element_type=jnp.float32)
        gating = jax.nn.sigmoid(jnp.dot(normed_row, gate_weight, preferred_element_type=jnp.float32))
        return (pair_row.astype(jnp.float32) + gating * projected).astype(jnp.bfloat16)
    return lax.map(one_row, (by_rows, current, normed))

def reference(pair_map, pair_mask, edge_weights, gate_weights, out_weights, norm_gains):
    normed, left_edges, right_edges = edge_maps(pair_map, pair_mask, edge_weights[0], norm_gains[0, 0])
    product_map = lax.map(lambda pair_items: jnp.dot(pair_items[0], pair_items[1].T, preferred_element_type=jnp.float32).astype(jnp.bfloat16), (left_edges, right_edges))
    current = finish(pair_map, normed, product_map, norm_gains[0, 1], out_weights[0], gate_weights[0])
    normed, left_edges, right_edges = edge_maps(current, pair_mask, edge_weights[1], norm_gains[1, 0])
    product_map = lax.map(lambda pair_items: jnp.dot(pair_items[0].T, pair_items[1], preferred_element_type=jnp.float32).astype(jnp.bfloat16), (left_edges, right_edges))
    return finish(current, normed, product_map, norm_gains[1, 1], out_weights[1], gate_weights[1])
```

```python
import functools

import jax
import jax.numpy as jnp
from jax import lax
from jax.experimental import pallas as pl
from jax.experimental.pallas import tpu as pltpu
from jax.sharding import PartitionSpec as P

BF = jnp.bfloat16
F32 = jnp.float32
MESH = pl.DeviceIdType.MESH


def dot(a, b, ca, cb):
    return lax.dot_general(a, b, (((ca,), (cb,)), ((), ())), preferred_element_type=F32)


def one_hot(source):
    rows = lax.broadcasted_iota(jnp.int32, (256, 256), 0)
    cols = lax.broadcasted_iota(jnp.int32, (256, 256), 1)
    return jnp.where(cols == source(rows), 1.0, 0.0).astype(BF)


def where_am_i():
    dap = lax.axis_index("dap")
    grp = lax.axis_index("grp")
    core = dap % 2
    x = (dap // 2) % 4
    y = (dap // 8) % 4
    zlo = dap // 32
    return x, y, zlo, grp, core


def device(x, y, zlo, zhi, core):
    return (((zlo * 4 + y) * 4 + x) * 2 + core, zhi)


def far_first(k, size):
    return (size // 2 + jnp.where(k % 2 == 1, size - (k + 1) // 2, k // 2)) % size


def kernel(z_ref, mask_ref, we_ref, wg_ref, wo_ref, gains_ref, out_ref,
           wt, perms, normed, cur, edges, send1, recv1, left, right, leftx, prod, send2, recv2, chan,
           s1, r1, s2, r2, sx, rx):
    x, y, zlo, zhi, core = where_am_i()
    slot = ((y * 4 + x) * 2 + core) * 4 + zhi
    channel = ((zlo * 4 + y) * 4 + x) * 4 + zhi
    sibling = device(x, y, zlo, zhi, 1 - core)

    barrier = pltpu.get_barrier_semaphore()

    def partner(i):
        tc, k = i % 2, i // 2
        tg = (zhi + far_first(k // 16, 4)) % 4
        tx = (x + far_first(k % 4, 4)) % 4
        ty = (y + far_first((k // 4) % 4, 4)) % 4
        return tx, ty, tg, tc

    def greet(i, carry):
        tx, ty, tg, tc = partner(i)

        @pl.when(jnp.logical_not((tx == x) & (ty == y) & (tg == zhi) & (zlo == core)))
        def _():
            pl.semaphore_signal(barrier, inc=1, device_id=device(tx, ty, core, tg, tc), device_id_type=MESH)

        return carry

    pl.semaphore_signal(barrier, inc=1, device_id=sibling, device_id_type=MESH)
    lax.fori_loop(0, 128, greet, 0)

    for u in range(2):
        wt[u] = we_ref[u].astype(F32).T.astype(BF)
    perms[0] = one_hot(lambda r: (r % 16) * 16 + r // 16)
    perms[1] = one_hot(lambda r: ((r // 2) % 16) * 16 + (r // 128) * 8 + (r % 2) * 4 + (r // 32) % 4)
    perms[2] = one_hot(lambda r: (r % 4) * 64 + r // 4)
    perms[3] = one_hot(lambda r: (r % 32) * 8 + r // 32)

    def project(u, source):
        gain = gains_ref[u, 0:1, :]
        for p in range(4):
            row, half = p // 2, p % 2
            lanes = slice(half * 256, half * 256 + 256)
            zf = source[row, lanes, :].astype(F32)
            centred = zf - jnp.mean(zf, axis=1, keepdims=True)
            variance = jnp.mean(centred * centred, axis=1, keepdims=True)
            nb = (centred * lax.rsqrt(variance + 1e-05) * gain).astype(BF)
            normed[u, row, lanes, :] = nb
            mask = mask_ref[row : row + 1, lanes].astype(F32)
            for lr in range(2):
                proj = dot(wt[u, lr * 256 : lr * 256 + 256, :], nb, 1, 1)
                edge = jax.nn.sigmoid(proj[:128]) * proj[128:] * mask
                edges[lr, :, p * 256 : p * 256 + 256] = edge.astype(BF)
        for b in range(8):
            rows = slice(b * 16, b * 16 + 16)
            stack = jnp.concatenate(
                [edges[lr, rows, j * 128 : j * 128 + 128] for lr in range(2) for j in range(8)], axis=0
            )
            tiles = dot(perms[0], stack, 1, 0).astype(BF)
            send1[u, rows] = tiles.reshape(16, 16, 128)

    def scatter_edges(u):
        def one(i, carry):
            k = i // 16
            tz = (2 * zhi + zlo + far_first(k, 8)) % 8
            tx = (x + far_first(i % 4, 4)) % 4
            ty = (y + far_first((i // 4) % 4, 4)) % 4
            tl, tg = tz % 2, tz // 2
            h = ((tl * 4 + ty) * 4 + tx) * 4 + tg
            own = (h == channel) & (zlo == core)

            @pl.when(jnp.logical_not(own))
            def _():
                pltpu.make_async_remote_copy(
                    src_ref=send1.at[u, h], dst_ref=recv1.at[u, slot], send_sem=s1.at[u], recv_sem=r1.at[u],
                    device_id=device(tx, ty, tl, tg, zlo), device_id_type=MESH,
                ).start()

            @pl.when(own)
            def _():
                pltpu.make_async_copy(send1.at[u, h], recv1.at[u, slot], r1.at[u]).start()

            return carry

        lax.fori_loop(0, 128, one, 0)

    def scatter_products(u):
        def one(i, carry):
            tx, ty, tg, tc = partner(i)
            at = ((ty * 4 + tx) * 2 + tc) * 4 + tg
            own = (at == slot) & (zlo == core)

            @pl.when(jnp.logical_not(own))
            def _():
                pltpu.make_async_remote_copy(
                    src_ref=send2.at[u, at], dst_ref=recv2.at[u, channel], send_sem=s2.at[u], recv_sem=r2.at[u],
                    device_id=device(tx, ty, core, tg, tc), device_id_type=MESH,
                ).start()

            @pl.when(own)
            def _():
                pltpu.make_async_copy(send2.at[u, at], recv2.at[u, channel], r2.at[u]).start()

            return carry

        lax.fori_loop(0, 128, one, 0)

    def wait_all(buf, sem):
        pltpu.make_async_copy(buf, buf, sem).wait()

    def to_sibling(src, dst, i):
        copy = pltpu.make_async_remote_copy(
            src_ref=src, dst_ref=dst, send_sem=sx.at[i], recv_sem=rx.at[i], device_id=sibling, device_id_type=MESH
        )
        copy.start()
        return copy

    def multiply(u):
        wait_all(recv1.at[u], r1.at[u])
        for b in range(8):
            block = recv1[u, b * 16 : b * 16 + 16].reshape(256, 128)
            sorted_ = dot(perms[1], block, 1, 0).astype(BF)
            rows = slice(b * 32, b * 32 + 32)
            for k in range(4):
                lanes = slice(k * 128, k * 128 + 128)
                right[u, core, rows, lanes] = sorted_[128 + k * 32 : 160 + k * 32]
                if u == 0:
                    left[k // 2, rows, (k % 2) * 128 : (k % 2) * 128 + 128] = sorted_[k * 32 : k * 32 + 32]
                else:
                    left[2 + k // 2, rows, (k % 2) * 128 : (k % 2) * 128 + 128] = sorted_[k * 32 : k * 32 + 32]
        copies = [to_sibling(right.at[u, core], right.at[u, core], u)]
        if u == 1:
            copies.append(to_sibling(left.at[2 + 1 - core], leftx, 2))
        if u == 0:
            for step in range(2):
                if step == 1:
                    copies[0].wait_recv()
                half = core if step == 0 else 1 - core
                rhs = right[u, half]
                total = dot(left[0], rhs[:, :256], 1, 1) + dot(left[1], rhs[:, 256:], 1, 1)
                prod[half] = total.astype(BF)
        else:
            mine = left[2 + core]
            totals = [dot(mine, right[u, core, :, j * 256 : j * 256 + 256], 0, 0) for j in range(2)]
            for copy in copies:
                copy.wait_recv()
            for j in range(2):
                other = dot(leftx[...], right[u, 1 - core, :, j * 256 : j * 256 + 256], 0, 0)
                prod[j] = (totals[j] + other).astype(BF)
        for b in range(4):
            rows = slice(b * 64, b * 64 + 64)
            stack = jnp.concatenate(
                [prod[j // 2, rows, (j % 2) * 128 : (j % 2) * 128 + 128] for j in range(4)], axis=0
            )
            tiles = dot(perms[2], stack, 1, 0).reshape(32, 8, 128)
            send2[u, b * 32 : b * 32 + 32] = tiles.astype(BF)
        return copies

    def finish(u, source, target):
        wait_all(recv2.at[u], r2.at[u])
        for b in range(4):
            block = recv2[u, b * 32 : b * 32 + 32].astype(F32).reshape(256, 128).astype(BF)
            tiles = dot(perms[3], block, 1, 0).astype(BF)
            for j in range(8):
                chan[b * 32 : b * 32 + 32, j * 128 : j * 128 + 128] = tiles[j * 32 : j * 32 + 32]
        gain = gains_ref[u, 1:2, :].reshape(128, 1)
        for p in range(4):
            row, half = p // 2, p % 2
            lanes = slice(half * 256, half * 256 + 256)
            values = chan[:, p * 256 : p * 256 + 256].astype(F32)
            centred = values - jnp.mean(values, axis=0, keepdims=True)
            variance = jnp.mean(centred * centred, axis=0, keepdims=True)
            scaled = (centred * lax.rsqrt(variance + 1e-05) * gain).astype(BF)
            projected = dot(scaled, wo_ref[u], 0, 0)
            gating = jax.nn.sigmoid(dot(normed[u, row, lanes, :], wg_ref[u], 1, 0))
            result = source[row, lanes, :].astype(F32) + gating * projected
            target[row, lanes, :] = result.astype(BF)

    copies = []
    for u in range(2):
        source, target = (z_ref, cur) if u == 0 else (cur, out_ref)
        project(u, source)
        if u == 0:
            pl.semaphore_wait(barrier, 128)
        scatter_edges(u)
        copies += multiply(u)
        scatter_products(u)
        finish(u, source, target)

    for copy in copies:
        copy.wait_send()
    for u in range(2):

        @pl.when(zlo == core)
        def _():
            wait_all(send1.at[u, pl.ds(0, 127)], s1.at[u])
            wait_all(send2.at[u, pl.ds(0, 127)], s2.at[u])

        @pl.when(zlo != core)
        def _():
            wait_all(send1.at[u], s1.at[u])
            wait_all(send2.at[u], s2.at[u])


def per_device(pair_map, pair_mask, edge_weights, gate_weights, out_weights, norm_gains):
    vmem = pl.BlockSpec(memory_space=pltpu.VMEM)
    return pl.pallas_call(
        kernel,
        out_shape=jax.ShapeDtypeStruct((2, 512, 128), BF),
        in_specs=[vmem] * 6,
        out_specs=vmem,
        scratch_shapes=[
            pltpu.VMEM((2, 512, 128), BF),
            pltpu.VMEM((4, 256, 256), BF),
            pltpu.VMEM((2, 2, 512, 128), BF),
            pltpu.VMEM((2, 512, 128), BF),
            pltpu.VMEM((2, 128, 1024), BF),
            pltpu.VMEM((2, 128, 16, 128), BF),
            pltpu.VMEM((2, 128, 16, 128), BF),
            pltpu.VMEM((4, 256, 256), BF),
            pltpu.VMEM((2, 2, 256, 512), BF),
            pltpu.VMEM((256, 256), BF),
            pltpu.VMEM((2, 256, 256), BF),
            pltpu.VMEM((2, 128, 8, 128), BF),
            pltpu.VMEM((2, 128, 8, 128), BF),
            pltpu.VMEM((128, 1024), BF),
            pltpu.SemaphoreType.DMA((2,)),
            pltpu.SemaphoreType.DMA((2,)),
            pltpu.SemaphoreType.DMA((2,)),
            pltpu.SemaphoreType.DMA((2,)),
            pltpu.SemaphoreType.DMA((3,)),
            pltpu.SemaphoreType.DMA((3,)),
        ],
        compiler_params=pltpu.CompilerParams(
            collective_id=0, has_side_effects=True, vmem_limit_bytes=40 * 1024 * 1024
        ),
        name="triangles",
    )(pair_map, pair_mask, edge_weights, gate_weights, out_weights, norm_gains)


def solution(mesh):
    return jax.shard_map(
        per_device,
        mesh=mesh,
        in_specs=(P(("dap", "grp"), None, None), P(("dap", "grp"), None), P(), P(), P(), P()),
        out_specs=P(("dap", "grp"), None, None),
        check_vma=False,
    )
```

```python
import functools

import jax
import jax.numpy as jnp
from jax import lax
from jax.experimental import pallas as pl
from jax.experimental.pallas import tpu as pltpu
from jax.sharding import PartitionSpec as P

BF = jnp.bfloat16
F32 = jnp.float32
MESH = pl.DeviceIdType.MESH


def dot(a, b, ca, cb):
    return lax.dot_general(a, b, (((ca,), (cb,)), ((), ())), preferred_element_type=F32)


def one_hot(source):
    rows = lax.broadcasted_iota(jnp.int32, (256, 256), 0)
    cols = lax.broadcasted_iota(jnp.int32, (256, 256), 1)
    return jnp.where(cols == source(rows), 1.0, 0.0).astype(BF)


def where_am_i():
    dap = lax.axis_index("dap")
    grp = lax.axis_index("grp")
    core = dap % 2
    x = (dap // 2) % 4
    y = (dap // 8) % 4
    zlo = dap // 32
    return x, y, zlo, grp, core


def device(x, y, zlo, zhi, core):
    return (((zlo * 4 + y) * 4 + x) * 2 + core, zhi)


XY = sorted(range(16), key=lambda o: (-(2 - abs(o % 4 - 2)) - (2 - abs(o // 4 - 2)), o))
XY_WORDS = [sum(o << (4 * i) for i, o in enumerate(XY[w : w + 7])) for w in (0, 7, 14)]


def xy_offset(i):
    word = jnp.where(i < 7, XY_WORDS[0], jnp.where(i < 14, XY_WORDS[1], XY_WORDS[2]))
    o = (word >> (4 * (i % 7))) % 16
    return o % 4, o // 4


def all_offset(i):
    j = i - 16
    ends = (j < 0) | (j >= 96)
    far = 3 - j // 32
    dz = jnp.where(j < 0, 4, jnp.where(j >= 96, 0, jnp.where(j % 2 == 1, 8 - far, far)))
    dx, dy = xy_offset(jnp.where(ends, i % 16, (j % 32) // 2))
    return dx, dy, dz


def half_offset(i, odd):
    m = jnp.where(odd, i, i - 16)
    single = jnp.logical_not(odd) & ((m < 0) | (m >= 32))
    far = jnp.where(odd, 3 - 2 * (i // 32), jnp.where(m < 0, 4, jnp.where(m >= 32, 0, 2)))
    dz = jnp.where(jnp.logical_not(single) & (i % 2 == 1), 8 - far, far)
    dx, dy = xy_offset(jnp.where(single, i % 16, (m % 32) // 2))
    return dx, dy, dz


def kernel(z_hbm, mask_hbm, we_hbm, wg_hbm, wo_hbm, gains_hbm, out_ref,
           z_ref, mask_ref, we_ref, wg_ref, wo_ref, gains_ref, wt, perms, normed, cur, edges, send1, recv1, left, right, leftx, prod, send2, recv2, chan,
           s1, r1, s2, r2, sx, rx, load):
    x, y, zlo, zhi, core = where_am_i()
    slot = ((y * 4 + x) * 2 + core) * 4 + zhi
    channel = ((zlo * 4 + y) * 4 + x) * 4 + zhi
    sibling = device(x, y, zlo, zhi, 1 - core)

    loads = [
        pltpu.make_async_copy(src, dst, load.at[i])
        for i, (src, dst) in enumerate(
            ((z_hbm, z_ref), (we_hbm, we_ref), (gains_hbm, gains_ref), (mask_hbm, mask_ref),
             (wg_hbm, wg_ref), (wo_hbm, wo_ref))
        )
    ]
    for copy in loads:
        copy.start()

    barrier = pltpu.get_barrier_semaphore()

    def partner(i):
        dx, dy, dz = half_offset(i % 64, zlo != core)
        return (x + dx) % 4, (y + dy) % 4, ((2 * zhi + zlo + dz) % 8) // 2, i // 64

    def greet(i, carry):
        tx, ty, tg, tc = partner(i)

        @pl.when(jnp.logical_not((tx == x) & (ty == y) & (tg == zhi) & (zlo == core)))
        def _():
            pl.semaphore_signal(barrier, inc=1, device_id=device(tx, ty, core, tg, tc), device_id_type=MESH)

        return carry

    pl.semaphore_signal(barrier, inc=1, device_id=sibling, device_id_type=MESH)
    lax.fori_loop(0, 128, greet, 0)

    perms[0] = one_hot(lambda r: (r % 16) * 16 + r // 16)
    perms[1] = one_hot(lambda r: ((r // 2) % 16) * 16 + (r // 128) * 8 + (r % 2) * 4 + (r // 32) % 4)
    perms[2] = one_hot(lambda r: (r % 4) * 64 + r // 4)
    perms[3] = one_hot(lambda r: (r % 32) * 8 + r // 32)

    for copy in loads:
        copy.wait()
    for u in range(2):
        wt[u] = we_ref[u].astype(F32).T.astype(BF)

    def project(u, source):
        gain = gains_ref[u, 0:1, :]
        for p in range(4):
            row, half = p // 2, p % 2
            lanes = slice(half * 256, half * 256 + 256)
            zf = source[row, lanes, :].astype(F32)
            centred = zf - jnp.mean(zf, axis=1, keepdims=True)
            variance = jnp.mean(centred * centred, axis=1, keepdims=True)
            nb = (centred * lax.rsqrt(variance + 1e-05) * gain).astype(BF)
            normed[u, row, lanes, :] = nb
            mask = mask_ref[row : row + 1, lanes].astype(F32)
            for lr in range(2):
                proj = dot(wt[u, lr * 256 : lr * 256 + 256, :], nb, 1, 1)
                edge = jax.nn.sigmoid(proj[:128]) * proj[128:] * mask
                edges[lr, :, p * 256 : p * 256 + 256] = edge.astype(BF)
        for b in range(8):
            rows = slice(b * 16, b * 16 + 16)
            stack = jnp.concatenate(
                [edges[lr, rows, j * 128 : j * 128 + 128] for lr in range(2) for j in range(8)], axis=0
            )
            tiles = dot(perms[0], stack, 1, 0).astype(BF)
            send1[u, rows] = tiles.reshape(16, 16, 128)

    def scatter_edges(u):
        def one(i, carry):
            dx, dy, dz = all_offset(i)
            tx, ty, tz = (x + dx) % 4, (y + dy) % 4, (2 * zhi + zlo + dz) % 8
            tl, tg = tz % 2, tz // 2
            h = ((tl * 4 + ty) * 4 + tx) * 4 + tg
            own = (h == channel) & (zlo == core)

            @pl.when(jnp.logical_not(own))
            def _():
                pltpu.make_async_remote_copy(
                    src_ref=send1.at[u, h], dst_ref=recv1.at[u, slot], send_sem=s1.at[u], recv_sem=r1.at[u],
                    device_id=device(tx, ty, tl, tg, zlo), device_id_type=MESH,
                ).start()

            @pl.when(own)
            def _():
                pltpu.make_async_copy(send1.at[u, h], recv1.at[u, slot], r1.at[u]).start()

            return carry

        lax.fori_loop(0, 128, one, 0)

    def scatter_products(u):
        def one(i, carry):
            tx, ty, tg, tc = partner(i)
            at = ((ty * 4 + tx) * 2 + tc) * 4 + tg
            own = (at == slot) & (zlo == core)

            @pl.when(jnp.logical_not(own))
            def _():
                pltpu.make_async_remote_copy(
                    src_ref=send2.at[u, at], dst_ref=recv2.at[u, channel], send_sem=s2.at[u], recv_sem=r2.at[u],
                    device_id=device(tx, ty, core, tg, tc), device_id_type=MESH,
                ).start()

            @pl.when(own)
            def _():
                pltpu.make_async_copy(send2.at[u, at], recv2.at[u, channel], r2.at[u]).start()

            return carry

        lax.fori_loop(0, 128, one, 0)

    def wait_all(buf, sem):
        pltpu.make_async_copy(buf, buf, sem).wait()

    def to_sibling(src, dst, i):
        copy = pltpu.make_async_remote_copy(
            src_ref=src, dst_ref=dst, send_sem=sx.at[i], recv_sem=rx.at[i], device_id=sibling, device_id_type=MESH
        )
        copy.start()
        return copy

    def multiply(u):
        wait_all(recv1.at[u], r1.at[u])
        for b in range(8):
            block = recv1[u, b * 16 : b * 16 + 16].reshape(256, 128)
            sorted_ = dot(perms[1], block, 1, 0).astype(BF)
            rows = slice(b * 32, b * 32 + 32)
            for k in range(4):
                lanes = slice(k * 128, k * 128 + 128)
                right[u, core, rows, lanes] = sorted_[128 + k * 32 : 160 + k * 32]
                if u == 0:
                    left[k // 2, rows, (k % 2) * 128 : (k % 2) * 128 + 128] = sorted_[k * 32 : k * 32 + 32]
                else:
                    left[2 + k // 2, rows, (k % 2) * 128 : (k % 2) * 128 + 128] = sorted_[k * 32 : k * 32 + 32]
        copies = [to_sibling(right.at[u, core], right.at[u, core], u)]
        if u == 1:
            copies.append(to_sibling(left.at[2 + 1 - core], leftx, 2))
        if u == 0:
            for step in range(2):
                if step == 1:
                    copies[0].wait_recv()
                half = core if step == 0 else 1 - core
                rhs = right[u, half]
                total = dot(left[0], rhs[:, :256], 1, 1) + dot(left[1], rhs[:, 256:], 1, 1)
                prod[half] = total.astype(BF)
        else:
            mine = left[2 + core]
            totals = [dot(mine, right[u, core, :, j * 256 : j * 256 + 256], 0, 0) for j in range(2)]
            for copy in copies:
                copy.wait_recv()
            for j in range(2):
                other = dot(leftx[...], right[u, 1 - core, :, j * 256 : j * 256 + 256], 0, 0)
                prod[j] = (totals[j] + other).astype(BF)
        for b in range(4):
            rows = slice(b * 64, b * 64 + 64)
            stack = jnp.concatenate(
                [prod[j // 2, rows, (j % 2) * 128 : (j % 2) * 128 + 128] for j in range(4)], axis=0
            )
            tiles = dot(perms[2], stack, 1, 0).reshape(32, 8, 128)
            send2[u, b * 32 : b * 32 + 32] = tiles.astype(BF)
        return copies

    def finish(u, source, target):
        wait_all(recv2.at[u], r2.at[u])
        for b in range(4):
            block = recv2[u, b * 32 : b * 32 + 32].astype(F32).reshape(256, 128).astype(BF)
            tiles = dot(perms[3], block, 1, 0).astype(BF)
            for j in range(8):
                chan[b * 32 : b * 32 + 32, j * 128 : j * 128 + 128] = tiles[j * 32 : j * 32 + 32]
        gain = gains_ref[u, 1:2, :].reshape(128, 1)
        for p in range(4):
            row, half = p // 2, p % 2
            lanes = slice(half * 256, half * 256 + 256)
            values = chan[:, p * 256 : p * 256 + 256].astype(F32)
            centred = values - jnp.mean(values, axis=0, keepdims=True)
            variance = jnp.mean(centred * centred, axis=0, keepdims=True)
            scaled = (centred * lax.rsqrt(variance + 1e-05) * gain).astype(BF)
            projected = dot(scaled, wo_ref[u], 0, 0)
            gating = jax.nn.sigmoid(dot(normed[u, row, lanes, :], wg_ref[u], 1, 0))
            result = source[row, lanes, :].astype(F32) + gating * projected
            target[row, lanes, :] = result.astype(BF)

    copies = []
    for u in range(2):
        source, target = (z_ref, cur) if u == 0 else (cur, out_ref)
        project(u, source)
        if u == 0:
            pl.semaphore_wait(barrier, 128)
        scatter_edges(u)
        copies += multiply(u)
        scatter_products(u)
        finish(u, source, target)

    for copy in copies:
        copy.wait_send()
    for u in range(2):

        @pl.when(zlo == core)
        def _():
            wait_all(send1.at[u, pl.ds(0, 127)], s1.at[u])
            wait_all(send2.at[u, pl.ds(0, 127)], s2.at[u])

        @pl.when(zlo != core)
        def _():
            wait_all(send1.at[u], s1.at[u])
            wait_all(send2.at[u], s2.at[u])


def per_device(pair_map, pair_mask, edge_weights, gate_weights, out_weights, norm_gains):
    vmem = pl.BlockSpec(memory_space=pltpu.VMEM)
    return pl.pallas_call(
        kernel,
        out_shape=jax.ShapeDtypeStruct((2, 512, 128), BF),
        in_specs=[pl.BlockSpec(memory_space=pl.ANY)] * 6,
        out_specs=vmem,
        scratch_shapes=[
            pltpu.VMEM((2, 512, 128), BF),
            pltpu.VMEM((2, 512), jnp.int32),
            pltpu.VMEM((2, 128, 512), BF),
            pltpu.VMEM((2, 128, 128), BF),
            pltpu.VMEM((2, 128, 128), BF),
            pltpu.VMEM((2, 2, 128), F32),
            pltpu.VMEM((2, 512, 128), BF),
            pltpu.VMEM((4, 256, 256), BF),
            pltpu.VMEM((2, 2, 512, 128), BF),
            pltpu.VMEM((2, 512, 128), BF),
            pltpu.VMEM((2, 128, 1024), BF),
            pltpu.VMEM((2, 128, 16, 128), BF),
            pltpu.VMEM((2, 128, 16, 128), BF),
            pltpu.VMEM((4, 256, 256), BF),
            pltpu.VMEM((2, 2, 256, 512), BF),
            pltpu.VMEM((256, 256), BF),
            pltpu.VMEM((2, 256, 256), BF),
            pltpu.VMEM((2, 128, 8, 128), BF),
            pltpu.VMEM((2, 128, 8, 128), BF),
            pltpu.VMEM((128, 1024), BF),
            pltpu.SemaphoreType.DMA((2,)),
            pltpu.SemaphoreType.DMA((2,)),
            pltpu.SemaphoreType.DMA((2,)),
            pltpu.SemaphoreType.DMA((2,)),
            pltpu.SemaphoreType.DMA((3,)),
            pltpu.SemaphoreType.DMA((3,)),
            pltpu.SemaphoreType.DMA((6,)),
        ],
        compiler_params=pltpu.CompilerParams(
            collective_id=0, has_side_effects=True, vmem_limit_bytes=40 * 1024 * 1024
        ),
        name="triangles",
    )(pair_map, pair_mask, edge_weights, gate_weights, out_weights, norm_gains)


def solution(mesh):
    return jax.shard_map(
        per_device,
        mesh=mesh,
        in_specs=(P(("dap", "grp"), None, None), P(("dap", "grp"), None), P(), P(), P(), P()),
        out_specs=P(("dap", "grp"), None, None),
        check_vma=False,
    )
```

```python
import functools

import jax
import jax.numpy as jnp
from jax import lax
from jax.experimental import pallas as pl
from jax.experimental.pallas import tpu as pltpu
from jax.sharding import PartitionSpec as P

BF = jnp.bfloat16
F32 = jnp.float32
MESH = pl.DeviceIdType.MESH


def dot(a, b, ca, cb):
    return lax.dot_general(a, b, (((ca,), (cb,)), ((), ())), preferred_element_type=F32)


def one_hot(source):
    rows = lax.broadcasted_iota(jnp.int32, (256, 256), 0)
    cols = lax.broadcasted_iota(jnp.int32, (256, 256), 1)
    return jnp.where(cols == source(rows), 1.0, 0.0).astype(BF)


def ring(mask):
    return (0, 1, 2, 1)[mask]


XY_MASKS = sorted(((x, y) for x in range(4) for y in range(4)), key=lambda m: -ring(m[0]) - ring(m[1]))
Z_MASKS = (4, 5, 7, 3, 2, 6, 1, 0)
Z_EVEN = (4, 2, 6, 0)
Z_ODD = (5, 7, 3, 1)


def packed(masks):
    return sum((((m & 1) << 3) | (m >> 1)) << (4 * i) for i, m in enumerate(masks) if i < 7)


def nibble(word, i):
    return (word >> (4 * i)) & 15


def mesh_id(number):
    return (number >> 2, number & 3)


def kernel(z_hbm, mask_hbm, we_hbm, wg_hbm, wo_hbm, gains_hbm, out_ref,
           z_ref, mask_ref, we_ref, wg_ref, wo_ref, gains_ref, wt, perms, normed, cur, edges, send1, recv1, left, right, leftx, prod, send2, recv2, chan,
           s1, r1, s2, r2, sx, rx, load):
    dap = lax.axis_index("dap")
    number = dap * 4 + lax.axis_index("grp")
    core = (number >> 2) & 1
    zlo = number >> 7
    slot = number & 127
    channel = ((number >> 3) << 2) | (number & 3)
    sibling = mesh_id(number ^ 4)

    loads = [
        pltpu.make_async_copy(src, dst, load.at[i])
        for i, (src, dst) in enumerate(
            ((z_hbm, z_ref), (we_hbm, we_ref), (gains_hbm, gains_ref), (mask_hbm, mask_ref),
             (wg_hbm, wg_ref), (wo_hbm, wo_ref))
        )
    ]
    for copy in loads:
        copy.start()

    barrier = pltpu.get_barrier_semaphore()

    def partners(visit):
        word = jnp.where(zlo == core, packed(Z_EVEN), packed(Z_ODD))
        chip = number - core * 4

        def one(k, carry):
            z = nibble(word, k & 3)
            base = chip ^ (((z >> 3) << 7) | (z & 3) | ((k >> 2) << 2))
            for mx, my in XY_MASKS:
                visit(base ^ (my << 5 | mx << 3))
            return carry

        lax.fori_loop(0, 8, one, 0)

    def greet(other):
        @pl.when((other | 4) != (number | 4))
        def _():
            pl.semaphore_signal(barrier, inc=1, device_id=mesh_id(other), device_id_type=MESH)

    pl.semaphore_signal(barrier, inc=1, device_id=sibling, device_id_type=MESH)
    partners(greet)

    perms[0] = one_hot(lambda r: (r % 16) * 16 + r // 16)
    perms[1] = one_hot(lambda r: ((r // 2) % 16) * 16 + (r // 128) * 8 + (r % 2) * 4 + (r // 32) % 4)
    perms[2] = one_hot(lambda r: (r % 4) * 64 + r // 4)
    perms[3] = one_hot(lambda r: (r % 32) * 8 + r // 32)

    for copy in loads:
        copy.wait()
    for u in range(2):
        wt[u] = we_ref[u].astype(F32).T.astype(BF)

    def project(u, source):
        gain = gains_ref[u, 0:1, :]
        for p in range(4):
            row, half = p // 2, p % 2
            lanes = slice(half * 256, half * 256 + 256)
            zf = source[row, lanes, :].astype(F32)
            centred = zf - jnp.mean(zf, axis=1, keepdims=True)
            variance = jnp.mean(centred * centred, axis=1, keepdims=True)
            nb = (centred * lax.rsqrt(variance + 1e-05) * gain).astype(BF)
            normed[u, row, lanes, :] = nb
            mask = mask_ref[row : row + 1, lanes].astype(F32)
            for lr in range(2):
                proj = dot(wt[u, lr * 256 : lr * 256 + 256, :], nb, 1, 1)
                edge = jax.nn.sigmoid(proj[:128]) * proj[128:] * mask
                edges[lr, :, p * 256 : p * 256 + 256] = edge.astype(BF)
        for b in range(8):
            rows = slice(b * 16, b * 16 + 16)
            stack = jnp.concatenate(
                [edges[lr, rows, j * 128 : j * 128 + 128] for lr in range(2) for j in range(8)], axis=0
            )
            tiles = dot(perms[0], stack, 1, 0).astype(BF)
            send1[u, rows] = tiles.reshape(16, 16, 128)

    def scatter_edges(u):
        base = (number - core * 4) | (zlo << 2)

        def one(k, carry):
            z = jnp.where(k == 7, 0, nibble(packed(Z_MASKS), k))
            for mx, my in XY_MASKS:
                other = base ^ (((z >> 3) << 7) | (z & 3) | (my << 5 | mx << 3))
                h = channel ^ (((z >> 3) << 6) | (z & 3) | (my << 4 | mx << 2))
                copy = pltpu.make_async_remote_copy(
                    src_ref=send1.at[u, h], dst_ref=recv1.at[u, slot], send_sem=s1.at[u], recv_sem=r1.at[u],
                    device_id=mesh_id(other), device_id_type=MESH,
                )
                if mx or my:
                    copy.start()
                    continue
                pl.when(other != number)(copy.start)

                @pl.when(other == number)
                def _():
                    pltpu.make_async_copy(send1.at[u, h], recv1.at[u, slot], r1.at[u]).start()

            return carry

        lax.fori_loop(0, 8, one, 0)

    def scatter_products(u):
        def send(other):
            at = other & 127

            @pl.when(other != number)
            def _():
                pltpu.make_async_remote_copy(
                    src_ref=send2.at[u, at], dst_ref=recv2.at[u, channel], send_sem=s2.at[u], recv_sem=r2.at[u],
                    device_id=mesh_id(other), device_id_type=MESH,
                ).start()

            @pl.when(other == number)
            def _():
                pltpu.make_async_copy(send2.at[u, at], recv2.at[u, channel], r2.at[u]).start()

        partners(send)

    def wait_all(buf, sem):
        pltpu.make_async_copy(buf, buf, sem).wait()

    def to_sibling(src, dst, i):
        copy = pltpu.make_async_remote_copy(
            src_ref=src, dst_ref=dst, send_sem=sx.at[i], recv_sem=rx.at[i], device_id=sibling, device_id_type=MESH
        )
        copy.start()
        return copy

    def multiply(u):
        wait_all(recv1.at[u], r1.at[u])
        for b in range(8):
            block = recv1[u, b * 16 : b * 16 + 16].reshape(256, 128)
            sorted_ = dot(perms[1], block, 1, 0).astype(BF)
            rows = slice(b * 32, b * 32 + 32)
            for k in range(4):
                lanes = slice(k * 128, k * 128 + 128)
                right[u, core, rows, lanes] = sorted_[128 + k * 32 : 160 + k * 32]
                if u == 0:
                    left[k // 2, rows, (k % 2) * 128 : (k % 2) * 128 + 128] = sorted_[k * 32 : k * 32 + 32]
                else:
                    left[2 + k // 2, rows, (k % 2) * 128 : (k % 2) * 128 + 128] = sorted_[k * 32 : k * 32 + 32]
        copies = [to_sibling(right.at[u, core], right.at[u, core], u)]
        if u == 1:
            copies.append(to_sibling(left.at[2 + 1 - core], leftx, 2))
        if u == 0:
            for step in range(2):
                if step == 1:
                    copies[0].wait_recv()
                half = core if step == 0 else 1 - core
                rhs = right[u, half]
                total = dot(left[0], rhs[:, :256], 1, 1) + dot(left[1], rhs[:, 256:], 1, 1)
                prod[half] = total.astype(BF)
        else:
            mine = left[2 + core]
            totals = [dot(mine, right[u, core, :, j * 256 : j * 256 + 256], 0, 0) for j in range(2)]
            for copy in copies:
                copy.wait_recv()
            for j in range(2):
                other = dot(leftx[...], right[u, 1 - core, :, j * 256 : j * 256 + 256], 0, 0)
                prod[j] = (totals[j] + other).astype(BF)
        for b in range(4):
            rows = slice(b * 64, b * 64 + 64)
            stack = jnp.concatenate(
                [prod[j // 2, rows, (j % 2) * 128 : (j % 2) * 128 + 128] for j in range(4)], axis=0
            )
            tiles = dot(perms[2], stack, 1, 0).reshape(32, 8, 128)
            send2[u, b * 32 : b * 32 + 32] = tiles.astype(BF)
        return copies

    def finish(u, source, target):
        wait_all(recv2.at[u], r2.at[u])
        for b in range(4):
            block = recv2[u, b * 32 : b * 32 + 32].astype(F32).reshape(256, 128).astype(BF)
            tiles = dot(perms[3], block, 1, 0).astype(BF)
            for j in range(8):
                chan[b * 32 : b * 32 + 32, j * 128 : j * 128 + 128] = tiles[j * 32 : j * 32 + 32]
        gain = gains_ref[u, 1:2, :].reshape(128, 1)
        for p in range(4):
            row, half = p // 2, p % 2
            lanes = slice(half * 256, half * 256 + 256)
            values = chan[:, p * 256 : p * 256 + 256].astype(F32)
            centred = values - jnp.mean(values, axis=0, keepdims=True)
            variance = jnp.mean(centred * centred, axis=0, keepdims=True)
            scaled = (centred * lax.rsqrt(variance + 1e-05) * gain).astype(BF)
            projected = dot(scaled, wo_ref[u], 0, 0)
            gating = jax.nn.sigmoid(dot(normed[u, row, lanes, :], wg_ref[u], 1, 0))
            result = source[row, lanes, :].astype(F32) + gating * projected
            target[row, lanes, :] = result.astype(BF)

    copies = []
    for u in range(2):
        source, target = (z_ref, cur) if u == 0 else (cur, out_ref)
        project(u, source)
        if u == 0:
            pl.semaphore_wait(barrier, 128)
        scatter_edges(u)
        copies += multiply(u)
        scatter_products(u)
        finish(u, source, target)

    for copy in copies:
        copy.wait_send()
    for u in range(2):

        @pl.when(zlo == core)
        def _():
            wait_all(send1.at[u, pl.ds(0, 127)], s1.at[u])
            wait_all(send2.at[u, pl.ds(0, 127)], s2.at[u])

        @pl.when(zlo != core)
        def _():
            wait_all(send1.at[u], s1.at[u])
            wait_all(send2.at[u], s2.at[u])


def per_device(pair_map, pair_mask, edge_weights, gate_weights, out_weights, norm_gains):
    vmem = pl.BlockSpec(memory_space=pltpu.VMEM)
    return pl.pallas_call(
        kernel,
        out_shape=jax.ShapeDtypeStruct((2, 512, 128), BF),
        in_specs=[pl.BlockSpec(memory_space=pl.ANY)] * 6,
        out_specs=vmem,
        scratch_shapes=[
            pltpu.VMEM((2, 512, 128), BF),
            pltpu.VMEM((2, 512), jnp.int32),
            pltpu.VMEM((2, 128, 512), BF),
            pltpu.VMEM((2, 128, 128), BF),
            pltpu.VMEM((2, 128, 128), BF),
            pltpu.VMEM((2, 2, 128), F32),
            pltpu.VMEM((2, 512, 128), BF),
            pltpu.VMEM((4, 256, 256), BF),
            pltpu.VMEM((2, 2, 512, 128), BF),
            pltpu.VMEM((2, 512, 128), BF),
            pltpu.VMEM((2, 128, 1024), BF),
            pltpu.VMEM((2, 128, 16, 128), BF),
            pltpu.VMEM((2, 128, 16, 128), BF),
            pltpu.VMEM((4, 256, 256), BF),
            pltpu.VMEM((2, 2, 256, 512), BF),
            pltpu.VMEM((256, 256), BF),
            pltpu.VMEM((2, 256, 256), BF),
            pltpu.VMEM((2, 128, 8, 128), BF),
            pltpu.VMEM((2, 128, 8, 128), BF),
            pltpu.VMEM((128, 1024), BF),
            pltpu.SemaphoreType.DMA((2,)),
            pltpu.SemaphoreType.DMA((2,)),
            pltpu.SemaphoreType.DMA((2,)),
            pltpu.SemaphoreType.DMA((2,)),
            pltpu.SemaphoreType.DMA((3,)),
            pltpu.SemaphoreType.DMA((3,)),
            pltpu.SemaphoreType.DMA((6,)),
        ],
        compiler_params=pltpu.CompilerParams(
            collective_id=0, has_side_effects=True, vmem_limit_bytes=40 * 1024 * 1024
        ),
        name="triangles",
    )(pair_map, pair_mask, edge_weights, gate_weights, out_weights, norm_gains)


def solution(mesh):
    return jax.shard_map(
        per_device,
        mesh=mesh,
        in_specs=(P(("dap", "grp"), None, None), P(("dap", "grp"), None), P(), P(), P(), P()),
        out_specs=P(("dap", "grp"), None, None),
        check_vma=False,
    )
```

```python
import functools

import jax
import jax.numpy as jnp
from jax import lax
from jax.experimental import pallas as pl
from jax.experimental.pallas import tpu as pltpu
from jax.sharding import PartitionSpec as P

BF = jnp.bfloat16
F32 = jnp.float32
MESH = pl.DeviceIdType.MESH


def dot(a, b, ca, cb):
    return lax.dot_general(a, b, (((ca,), (cb,)), ((), ())), preferred_element_type=F32)


def one_hot(source):
    rows = lax.broadcasted_iota(jnp.int32, (256, 256), 0)
    cols = lax.broadcasted_iota(jnp.int32, (256, 256), 1)
    return jnp.where(cols == source(rows), 1.0, 0.0).astype(BF)


def ring(mask):
    return (0, 1, 2, 1)[mask]


XY_MASKS = sorted(((x, y) for x in range(4) for y in range(4)), key=lambda m: -ring(m[0]) - ring(m[1]))
Z_MASKS = (4, 5, 7, 3, 2, 6, 1, 0)
Z_EVEN = (4, 2, 6, 0)
Z_ODD = (5, 7, 3, 1)


def packed(masks):
    return sum((((m & 1) << 3) | (m >> 1)) << (4 * i) for i, m in enumerate(masks) if i < 7)


def nibble(word, i):
    return (word >> (4 * i)) & 15


def mesh_id(number):
    return (number >> 2, number & 3)


def kernel(z_hbm, mask_hbm, we_hbm, wg_hbm, wo_hbm, gains_hbm, out_ref,
           z_ref, mask_ref, we_ref, wg_ref, wo_ref, gains_ref, wt, perms, normed, cur, edges, send1, recv1, left, right, leftx, prod, send2, recv2, chan,
           s1, r1, s2, r2, sx, rx, load):
    dap = lax.axis_index("dap")
    number = dap * 4 + lax.axis_index("grp")
    core = (number >> 2) & 1
    zlo = number >> 7
    slot = number & 127
    channel = ((number >> 3) << 2) | (number & 3)
    sibling = mesh_id(number ^ 4)

    loads = [
        pltpu.make_async_copy(src, dst, load.at[i])
        for i, (src, dst) in enumerate(
            ((z_hbm, z_ref), (we_hbm, we_ref), (gains_hbm, gains_ref), (mask_hbm, mask_ref),
             (wg_hbm, wg_ref), (wo_hbm, wo_ref))
        )
    ]
    for copy in loads:
        copy.start()

    barrier = pltpu.get_barrier_semaphore()

    def partners(visit):
        word = jnp.where(zlo == core, packed(Z_EVEN), packed(Z_ODD))
        chip = number - core * 4

        def one(k, carry):
            z = nibble(word, k & 3)
            base = chip ^ (((z >> 3) << 7) | (z & 3) | ((k >> 2) << 2))
            for mx, my in XY_MASKS:
                visit(base ^ (my << 5 | mx << 3))
            return carry

        lax.fori_loop(0, 8, one, 0)

    def greet(other):
        @pl.when((other | 4) != (number | 4))
        def _():
            pl.semaphore_signal(barrier, inc=1, device_id=mesh_id(other), device_id_type=MESH)

    pl.semaphore_signal(barrier, inc=1, device_id=sibling, device_id_type=MESH)
    partners(greet)

    perms[0] = one_hot(lambda r: (r % 8) * 32 + r // 8)
    perms[1] = one_hot(lambda r: ((r // 2) % 32) * 8 + (r % 2) * 4 + r // 64)
    perms[2] = one_hot(lambda r: (r % 4) * 64 + r // 4)
    perms[3] = one_hot(lambda r: (r % 32) * 8 + r // 32)

    for copy in loads:
        copy.wait()
    for u in range(2):
        wt[u] = we_ref[u].astype(F32).T.astype(BF)

    def normalize_rows(u, source):
        gain = gains_ref[u, 0:1, :]
        for p in range(4):
            row, lanes = p // 2, slice(p % 2 * 256, p % 2 * 256 + 256)
            zf = source[row, lanes, :].astype(F32)
            centred = zf - jnp.mean(zf, axis=1, keepdims=True)
            variance = jnp.mean(centred * centred, axis=1, keepdims=True)
            normed[u, row, lanes, :] = (centred * lax.rsqrt(variance + 1e-05) * gain).astype(BF)

    def project(u, lr):
        for p in range(4):
            row, lanes = p // 2, slice(p % 2 * 256, p % 2 * 256 + 256)
            mask = mask_ref[row : row + 1, lanes].astype(F32)
            proj = dot(wt[u, lr * 256 : lr * 256 + 256, :], normed[u, row, lanes, :], 1, 1)
            edge = jax.nn.sigmoid(proj[:128]) * proj[128:] * mask
            edges[lr, :, p * 256 : p * 256 + 256] = edge.astype(BF)
        for b in range(4):
            rows = slice(b * 32, b * 32 + 32)
            stack = jnp.concatenate([edges[lr, rows, j * 128 : j * 128 + 128] for j in range(8)], axis=0)
            send1[u, lr, rows] = dot(perms[0], stack, 1, 0).reshape(32, 8, 128).astype(BF)

    def scatter_edges(u, lr):
        base = (number - core * 4) | (zlo << 2)

        def one(k, carry):
            z = jnp.where(k == 7, 0, nibble(packed(Z_MASKS), k))
            for mx, my in XY_MASKS:
                other = base ^ (((z >> 3) << 7) | (z & 3) | (my << 5 | mx << 3))
                h = channel ^ (((z >> 3) << 6) | (z & 3) | (my << 4 | mx << 2))
                copy = pltpu.make_async_remote_copy(
                    src_ref=send1.at[u, lr, h], dst_ref=recv1.at[u, lr, slot], send_sem=s1.at[u, lr],
                    recv_sem=r1.at[u, lr],
                    device_id=mesh_id(other), device_id_type=MESH,
                )
                if mx or my:
                    copy.start()
                    continue
                pl.when(other != number)(copy.start)

                @pl.when(other == number)
                def _():
                    pltpu.make_async_copy(send1.at[u, lr, h], recv1.at[u, lr, slot], r1.at[u, lr]).start()

            return carry

        lax.fori_loop(0, 8, one, 0)

    def scatter_products(u):
        def send(other):
            at = other & 127

            @pl.when(other != number)
            def _():
                pltpu.make_async_remote_copy(
                    src_ref=send2.at[u, at], dst_ref=recv2.at[u, channel], send_sem=s2.at[u], recv_sem=r2.at[u],
                    device_id=mesh_id(other), device_id_type=MESH,
                ).start()

            @pl.when(other == number)
            def _():
                pltpu.make_async_copy(send2.at[u, at], recv2.at[u, channel], r2.at[u]).start()

        partners(send)

    def wait_all(buf, sem):
        pltpu.make_async_copy(buf, buf, sem).wait()

    def to_sibling(src, dst, i):
        copy = pltpu.make_async_remote_copy(
            src_ref=src, dst_ref=dst, send_sem=sx.at[i], recv_sem=rx.at[i], device_id=sibling, device_id_type=MESH
        )
        copy.start()
        return copy

    def gathered(u, lr, b):
        wanted = recv1[u, lr, b * 32 : b * 32 + 32].astype(F32).reshape(256, 128).astype(BF)
        blocks = dot(perms[1], wanted, 1, 0).astype(BF)
        return [blocks[k * 64 : k * 64 + 64] for k in range(4)]

    def multiply(u):
        wait_all(recv1.at[u, 1], r1.at[u, 1])
        for b in range(4):
            for k, block in enumerate(gathered(u, 1, b)):
                right[u, core, b * 64 : b * 64 + 64, k * 128 : k * 128 + 128] = block
        copies = [to_sibling(right.at[u, core], right.at[u, core], u)]
        wait_all(recv1.at[u, 0], r1.at[u, 0])
        for b in range(4):
            for k, block in enumerate(gathered(u, 0, b)):
                left[2 * u + k // 2, b * 64 : b * 64 + 64, k % 2 * 128 : k % 2 * 128 + 128] = block
        if u == 1:
            copies.append(to_sibling(left.at[2 + 1 - core], leftx, 2))
        if u == 0:
            for step in range(2):
                if step == 1:
                    copies[0].wait_recv()
                half = core if step == 0 else 1 - core
                rhs = right[u, half]
                total = dot(left[0], rhs[:, :256], 1, 1) + dot(left[1], rhs[:, 256:], 1, 1)
                prod[half] = total.astype(BF)
        else:
            mine = left[2 + core]
            totals = [dot(mine, right[u, core, :, j * 256 : j * 256 + 256], 0, 0) for j in range(2)]
            for copy in copies:
                copy.wait_recv()
            for j in range(2):
                other = dot(leftx[...], right[u, 1 - core, :, j * 256 : j * 256 + 256], 0, 0)
                prod[j] = (totals[j] + other).astype(BF)
        for b in range(4):
            rows = slice(b * 64, b * 64 + 64)
            stack = jnp.concatenate(
                [prod[j // 2, rows, (j % 2) * 128 : (j % 2) * 128 + 128] for j in range(4)], axis=0
            )
            tiles = dot(perms[2], stack, 1, 0).reshape(32, 8, 128)
            send2[u, b * 32 : b * 32 + 32] = tiles.astype(BF)
        return copies

    def finish(u, source, target):
        wait_all(recv2.at[u], r2.at[u])
        for b in range(4):
            block = recv2[u, b * 32 : b * 32 + 32].astype(F32).reshape(256, 128).astype(BF)
            tiles = dot(perms[3], block, 1, 0).astype(BF)
            for j in range(8):
                chan[b * 32 : b * 32 + 32, j * 128 : j * 128 + 128] = tiles[j * 32 : j * 32 + 32]
        gain = gains_ref[u, 1:2, :].reshape(128, 1)
        for p in range(4):
            row, half = p // 2, p % 2
            lanes = slice(half * 256, half * 256 + 256)
            values = chan[:, p * 256 : p * 256 + 256].astype(F32)
            centred = values - jnp.mean(values, axis=0, keepdims=True)
            variance = jnp.mean(centred * centred, axis=0, keepdims=True)
            scaled = (centred * lax.rsqrt(variance + 1e-05) * gain).astype(BF)
            projected = dot(scaled, wo_ref[u], 0, 0)
            gating = jax.nn.sigmoid(dot(normed[u, row, lanes, :], wg_ref[u], 1, 0))
            result = source[row, lanes, :].astype(F32) + gating * projected
            target[row, lanes, :] = result.astype(BF)

    copies = []
    for u in range(2):
        source, target = (z_ref, cur) if u == 0 else (cur, out_ref)
        normalize_rows(u, source)
        if u == 0:
            project(u, 1)
            project(u, 0)
            pl.semaphore_wait(barrier, 128)
            scatter_edges(u, 1)
            scatter_edges(u, 0)
        else:
            project(u, 1)
            scatter_edges(u, 1)
            project(u, 0)
            scatter_edges(u, 0)
        copies += multiply(u)
        scatter_products(u)
        finish(u, source, target)

    for copy in copies:
        copy.wait_send()
    for u in range(2):

        @pl.when(zlo == core)
        def _():
            for lr in range(2):
                wait_all(send1.at[u, lr, pl.ds(0, 127)], s1.at[u, lr])
            wait_all(send2.at[u, pl.ds(0, 127)], s2.at[u])

        @pl.when(zlo != core)
        def _():
            for lr in range(2):
                wait_all(send1.at[u, lr], s1.at[u, lr])
            wait_all(send2.at[u], s2.at[u])


def per_device(pair_map, pair_mask, edge_weights, gate_weights, out_weights, norm_gains):
    vmem = pl.BlockSpec(memory_space=pltpu.VMEM)
    return pl.pallas_call(
        kernel,
        out_shape=jax.ShapeDtypeStruct((2, 512, 128), BF),
        in_specs=[pl.BlockSpec(memory_space=pl.ANY)] * 6,
        out_specs=vmem,
        scratch_shapes=[
            pltpu.VMEM((2, 512, 128), BF),
            pltpu.VMEM((2, 512), jnp.int32),
            pltpu.VMEM((2, 128, 512), BF),
            pltpu.VMEM((2, 128, 128), BF),
            pltpu.VMEM((2, 128, 128), BF),
            pltpu.VMEM((2, 2, 128), F32),
            pltpu.VMEM((2, 512, 128), BF),
            pltpu.VMEM((4, 256, 256), BF),
            pltpu.VMEM((2, 2, 512, 128), BF),
            pltpu.VMEM((2, 512, 128), BF),
            pltpu.VMEM((2, 128, 1024), BF),
            pltpu.VMEM((2, 2, 128, 8, 128), BF),
            pltpu.VMEM((2, 2, 128, 8, 128), BF),
            pltpu.VMEM((4, 256, 256), BF),
            pltpu.VMEM((2, 2, 256, 512), BF),
            pltpu.VMEM((256, 256), BF),
            pltpu.VMEM((2, 256, 256), BF),
            pltpu.VMEM((2, 128, 8, 128), BF),
            pltpu.VMEM((2, 128, 8, 128), BF),
            pltpu.VMEM((128, 1024), BF),
            pltpu.SemaphoreType.DMA((2, 2)),
            pltpu.SemaphoreType.DMA((2, 2)),
            pltpu.SemaphoreType.DMA((2,)),
            pltpu.SemaphoreType.DMA((2,)),
            pltpu.SemaphoreType.DMA((3,)),
            pltpu.SemaphoreType.DMA((3,)),
            pltpu.SemaphoreType.DMA((6,)),
        ],
        compiler_params=pltpu.CompilerParams(
            collective_id=0, has_side_effects=True, vmem_limit_bytes=40 * 1024 * 1024
        ),
        name="triangles",
    )(pair_map, pair_mask, edge_weights, gate_weights, out_weights, norm_gains)


def solution(mesh):
    return jax.shard_map(
        per_device,
        mesh=mesh,
        in_specs=(P(("dap", "grp"), None, None), P(("dap", "grp"), None), P(), P(), P(), P()),
        out_specs=P(("dap", "grp"), None, None),
        check_vma=False,
    )
```

```python
import functools

import jax
import jax.numpy as jnp
from jax import lax
from jax.experimental import pallas as pl
from jax.experimental.pallas import tpu as pltpu
from jax.sharding import PartitionSpec as P

BF = jnp.bfloat16
F32 = jnp.float32
MESH = pl.DeviceIdType.MESH


def dot(a, b, ca, cb):
    return lax.dot_general(a, b, (((ca,), (cb,)), ((), ())), preferred_element_type=F32)


def one_hot(source):
    rows = lax.broadcasted_iota(jnp.int32, (256, 256), 0)
    cols = lax.broadcasted_iota(jnp.int32, (256, 256), 1)
    return jnp.where(cols == source(rows), 1.0, 0.0).astype(BF)


def ring(mask):
    return (0, 1, 2, 1)[mask]


XY_MASKS = sorted(((x, y) for x in range(4) for y in range(4)), key=lambda m: -ring(m[0]) - ring(m[1]))
Z_MASKS = (4, 5, 7, 3, 2, 6, 1, 0)
Z_EVEN = (4, 2, 6, 0)
Z_ODD = (5, 7, 3, 1)


def packed(masks):
    return sum((((m & 1) << 3) | (m >> 1)) << (4 * i) for i, m in enumerate(masks) if i < 7)


def nibble(word, i):
    return (word >> (4 * i)) & 15


def mesh_id(number):
    return (number >> 2, number & 3)


def kernel(z_hbm, mask_hbm, we_hbm, wg_hbm, wo_hbm, gains_hbm, out_ref,
           z_ref, mask_ref, we_ref, wg_ref, wo_ref, gains_ref, wt, perms, normed, cur, edges, send1, recv1, left, right, prod, send2, recv2,
           send3, recv3, pairs, send4, recv4, chan, s1, r1, s2, r2, s3, r3, s4, r4, sx, rx, load):
    dap = lax.axis_index("dap")
    number = dap * 4 + lax.axis_index("grp")
    core = (number >> 2) & 1
    zlo = number >> 7
    slot = number & 127
    channel = ((number >> 3) << 2) | (number & 3)
    sibling = mesh_id(number ^ 4)

    loads = [
        pltpu.make_async_copy(src, dst, load.at[i])
        for i, (src, dst) in enumerate(
            ((z_hbm, z_ref), (we_hbm, we_ref), (gains_hbm, gains_ref), (mask_hbm, mask_ref),
             (wg_hbm, wg_ref), (wo_hbm, wo_ref))
        )
    ]
    for copy in loads:
        copy.start()

    barrier = pltpu.get_barrier_semaphore()

    def partners(visit):
        word = jnp.where(zlo == core, packed(Z_EVEN), packed(Z_ODD))
        chip = number - core * 4

        def one(k, carry):
            z = nibble(word, k & 3)
            base = chip ^ (((z >> 3) << 7) | (z & 3) | ((k >> 2) << 2))
            for mx, my in XY_MASKS:
                visit(base ^ (my << 5 | mx << 3))
            return carry

        lax.fori_loop(0, 8, one, 0)

    def greet(other):
        @pl.when((other | 4) != (number | 4))
        def _():
            pl.semaphore_signal(barrier, inc=1, device_id=mesh_id(other), device_id_type=MESH)

    pl.semaphore_signal(barrier, inc=1, device_id=sibling, device_id_type=MESH)
    partners(greet)

    perms[0] = one_hot(lambda r: (r % 8) * 32 + r // 8)
    perms[1] = one_hot(lambda r: ((r // 2) % 32) * 8 + (r % 2) * 4 + r // 64)
    perms[4] = one_hot(lambda r: (r % 16) * 16 + r // 16)
    perms[5] = one_hot(lambda r: ((r // 2) % 16) * 16 + (r // 128) * 8 + (r % 2) * 4 + (r // 32) % 4)
    perms[2] = one_hot(lambda r: (r % 4) * 64 + r // 4)
    perms[3] = one_hot(lambda r: (r % 32) * 8 + r // 32)

    for copy in loads:
        copy.wait()
    for u in range(2):
        wt[u] = we_ref[u].astype(F32).T.astype(BF)

    def normalize_rows(u, source):
        gain = gains_ref[u, 0:1, :]
        for p in range(4):
            row, lanes = p // 2, slice(p % 2 * 256, p % 2 * 256 + 256)
            zf = source[row, lanes, :].astype(F32)
            centred = zf - jnp.mean(zf, axis=1, keepdims=True)
            variance = jnp.mean(centred * centred, axis=1, keepdims=True)
            normed[u, row, lanes, :] = (centred * lax.rsqrt(variance + 1e-05) * gain).astype(BF)

    def edge_map(u, lr):
        for p in range(4):
            row, lanes = p // 2, slice(p % 2 * 256, p % 2 * 256 + 256)
            mask = mask_ref[row : row + 1, lanes].astype(F32)
            proj = dot(wt[u, lr * 256 : lr * 256 + 256, :], normed[u, row, lanes, :], 1, 1)
            edge = jax.nn.sigmoid(proj[:128]) * proj[128:] * mask
            edges[lr, :, p * 256 : p * 256 + 256] = edge.astype(BF)

    def pack_one(lr):
        for b in range(4):
            rows = slice(b * 32, b * 32 + 32)
            stack = jnp.concatenate([edges[lr, rows, j * 128 : j * 128 + 128] for j in range(8)], axis=0)
            send1[lr, rows] = dot(perms[0], stack, 1, 0).reshape(32, 8, 128).astype(BF)

    def pack_both():
        for b in range(8):
            rows = slice(b * 16, b * 16 + 16)
            stack = jnp.concatenate(
                [edges[lr, rows, j * 128 : j * 128 + 128] for lr in range(2) for j in range(8)], axis=0
            )
            send3[rows] = dot(perms[4], stack, 1, 0).astype(BF).reshape(16, 16, 128)

    def scatter_edges(lr):
        base = (number - core * 4) | (zlo << 2)

        def one(k, carry):
            z = jnp.where(k == 7, 0, nibble(packed(Z_MASKS), k))
            for mx, my in XY_MASKS:
                other = base ^ (((z >> 3) << 7) | (z & 3) | (my << 5 | mx << 3))
                h = channel ^ (((z >> 3) << 6) | (z & 3) | (my << 4 | mx << 2))
                copy = pltpu.make_async_remote_copy(
                    src_ref=send1.at[lr, h], dst_ref=recv1.at[lr, slot], send_sem=s1.at[lr],
                    recv_sem=r1.at[lr],
                    device_id=mesh_id(other), device_id_type=MESH,
                )
                if mx or my:
                    copy.start()
                    continue
                pl.when(other != number)(copy.start)

                @pl.when(other == number)
                def _():
                    pltpu.make_async_copy(send1.at[lr, h], recv1.at[lr, slot], r1.at[lr]).start()

            return carry

        lax.fori_loop(0, 8, one, 0)

    def scatter_products():
        def send(other):
            at = other & 127

            @pl.when(other != number)
            def _():
                pltpu.make_async_remote_copy(
                    src_ref=send2.at[at], dst_ref=recv2.at[channel], send_sem=s2, recv_sem=r2,
                    device_id=mesh_id(other), device_id_type=MESH,
                ).start()

            @pl.when(other == number)
            def _():
                pltpu.make_async_copy(send2.at[at], recv2.at[channel], r2).start()

        partners(send)

    mine = ((number >> 2) << 1) | (number & 1)

    def scatter_pairs():
        z = ((number & 3) << 1) | zlo
        plane = number & (15 << 3)

        def one(k, carry):
            worker_core = k & 1
            step = k >> 1
            dz = jnp.where(step == 0, 2 + 4 * worker_core, jnp.where(step == 1, 1, jnp.where(step == 2, 7, 0)))
            wz = (z + dz) & 7
            base = ((wz & 1) << 7) | plane | (worker_core << 2) | (wz >> 1)
            for mx, my in XY_MASKS:
                other = base ^ (my << 5 | mx << 3)
                h = ((other >> 2) << 1) | (other & 1)
                copy = pltpu.make_async_remote_copy(
                    src_ref=send3.at[h], dst_ref=recv3.at[mine], send_sem=s3, recv_sem=r3,
                    device_id=mesh_id(other), device_id_type=MESH,
                )
                if mx or my:
                    copy.start()
                    continue
                pl.when(other != number)(copy.start)

                @pl.when(other == number)
                def _():
                    pltpu.make_async_copy(send3.at[h], recv3.at[mine], r3).start()

            return carry

        lax.fori_loop(0, 8, one, 0)

    def scatter_parts():
        part = (number >> 1) & 1

        def one(k, carry):
            zk = k >> 1
            z = jnp.where(zk == 7, 0, nibble(packed(Z_MASKS), zk))
            base = number ^ (((z >> 3) << 7) | (z & 3) | ((k & 1) << 2))
            for mx, my in XY_MASKS:
                other = base ^ (my << 5 | mx << 3)
                copy = pltpu.make_async_remote_copy(
                    src_ref=send4.at[other], dst_ref=recv4.at[part, mine], send_sem=s4, recv_sem=r4,
                    device_id=mesh_id(other), device_id_type=MESH,
                )
                if mx or my:
                    copy.start()
                    continue
                pl.when(other != number)(copy.start)

                @pl.when(other == number)
                def _():
                    pltpu.make_async_copy(send4.at[other], recv4.at[part, mine], r4).start()

            return carry

        lax.fori_loop(0, 16, one, 0)

    def wait_all(buf, sem):
        pltpu.make_async_copy(buf, buf, sem).wait()

    def gathered(lr, b):
        wanted = recv1[lr, b * 32 : b * 32 + 32].astype(F32).reshape(256, 128).astype(BF)
        blocks = dot(perms[1], wanted, 1, 0).astype(BF)
        return [blocks[k * 64 : k * 64 + 64] for k in range(4)]

    def messages(rows_of):
        stack = jnp.concatenate(rows_of, axis=0)
        return dot(perms[2], stack, 1, 0).reshape(32, 8, 128).astype(BF)

    def multiply_outgoing():
        wait_all(recv1.at[1], r1.at[1])
        for b in range(4):
            for k, block in enumerate(gathered(1, b)):
                right[core, b * 64 : b * 64 + 64, k * 128 : k * 128 + 128] = block
        relay = pltpu.make_async_remote_copy(
            src_ref=right.at[core], dst_ref=right.at[core], send_sem=sx, recv_sem=rx, device_id=sibling,
            device_id_type=MESH,
        )
        relay.start()
        wait_all(recv1.at[0], r1.at[0])
        for b in range(4):
            for k, block in enumerate(gathered(0, b)):
                left[b * 64 : b * 64 + 64, k * 128 : k * 128 + 128] = block
        for step in range(2):
            if step == 1:
                relay.wait_recv()
            half = core if step == 0 else 1 - core
            prod[half] = dot(left[...], right[half], 1, 1).astype(BF)
        for b in range(4):
            rows = slice(b * 64, b * 64 + 64)
            send2[b * 32 : b * 32 + 32] = messages(
                [prod[j // 2, rows, (j % 2) * 128 : (j % 2) * 128 + 128] for j in range(4)]
            )
        return relay

    def multiply_incoming():
        wait_all(recv3, r3)
        for b in range(8):
            wanted = recv3[b * 16 : b * 16 + 16].reshape(256, 128)
            blocks = dot(perms[5], wanted, 1, 0).astype(BF)
            for lr in range(2):
                for k in range(4):
                    pairs[lr, b * 32 : b * 32 + 32, k * 128 : k * 128 + 128] = blocks[
                        lr * 128 + k * 32 : lr * 128 + k * 32 + 32
                    ]
        for i in range(2):
            part = dot(pairs[0, :, i * 256 : i * 256 + 256], pairs[1], 0, 0).astype(BF)
            for b in range(4):
                send4[i * 128 + b * 32 : i * 128 + b * 32 + 32] = messages(
                    [part[b * 64 : b * 64 + 64, j * 128 : j * 128 + 128] for j in range(4)]
                )

    def by_channel(buf, b):
        block = buf[b * 32 : b * 32 + 32].astype(F32).reshape(256, 128).astype(BF)
        return dot(perms[3], block, 1, 0)

    def finish(u, source, target):
        if u == 0:
            wait_all(recv2, r2)
        else:
            wait_all(recv4, r4)
        for b in range(4):
            if u == 0:
                tiles = by_channel(recv2, b)
            else:
                tiles = by_channel(recv4.at[0], b) + by_channel(recv4.at[1], b)
            for j in range(8):
                chan[b * 32 : b * 32 + 32, j * 128 : j * 128 + 128] = tiles[j * 32 : j * 32 + 32]
        gain = gains_ref[u, 1:2, :].reshape(128, 1)
        for p in range(4):
            row, half = p // 2, p % 2
            lanes = slice(half * 256, half * 256 + 256)
            values = chan[:, p * 256 : p * 256 + 256]
            centred = values - jnp.mean(values, axis=0, keepdims=True)
            variance = jnp.mean(centred * centred, axis=0, keepdims=True)
            scaled = (centred * lax.rsqrt(variance + 1e-05) * gain).astype(BF)
            projected = dot(scaled, wo_ref[u], 0, 0)
            gating = jax.nn.sigmoid(dot(normed[u, row, lanes, :], wg_ref[u], 1, 0))
            result = source[row, lanes, :].astype(F32) + gating * projected
            target[row, lanes, :] = result.astype(BF)

    normalize_rows(0, z_ref)
    for lr in (1, 0):
        edge_map(0, lr)
        pack_one(lr)
    pl.semaphore_wait(barrier, 128)
    scatter_edges(1)
    scatter_edges(0)
    relay = multiply_outgoing()
    scatter_products()
    finish(0, z_ref, cur)

    normalize_rows(1, cur)
    edge_map(1, 0)
    edge_map(1, 1)
    pack_both()
    scatter_pairs()
    multiply_incoming()
    scatter_parts()
    finish(1, cur, out_ref)

    relay.wait_send()
    wait_all(send3.at[pl.ds(0, 127)], s3)
    wait_all(send4.at[pl.ds(0, 255)], s4)

    @pl.when(zlo == core)
    def _():
        for lr in range(2):
            wait_all(send1.at[lr, pl.ds(0, 127)], s1.at[lr])
        wait_all(send2.at[pl.ds(0, 127)], s2)

    @pl.when(zlo != core)
    def _():
        for lr in range(2):
            wait_all(send1.at[lr], s1.at[lr])
        wait_all(send2, s2)


def per_device(pair_map, pair_mask, edge_weights, gate_weights, out_weights, norm_gains):
    vmem = pl.BlockSpec(memory_space=pltpu.VMEM)
    return pl.pallas_call(
        kernel,
        out_shape=jax.ShapeDtypeStruct((2, 512, 128), BF),
        in_specs=[pl.BlockSpec(memory_space=pl.ANY)] * 6,
        out_specs=vmem,
        scratch_shapes=[
            pltpu.VMEM((2, 512, 128), BF),
            pltpu.VMEM((2, 512), jnp.int32),
            pltpu.VMEM((2, 128, 512), BF),
            pltpu.VMEM((2, 128, 128), BF),
            pltpu.VMEM((2, 128, 128), BF),
            pltpu.VMEM((2, 2, 128), F32),
            pltpu.VMEM((2, 512, 128), BF),
            pltpu.VMEM((6, 256, 256), BF),
            pltpu.VMEM((2, 2, 512, 128), BF),
            pltpu.VMEM((2, 512, 128), BF),
            pltpu.VMEM((2, 128, 1024), BF),
            pltpu.VMEM((2, 128, 8, 128), BF),
            pltpu.VMEM((2, 128, 8, 128), BF),
            pltpu.VMEM((256, 512), BF),
            pltpu.VMEM((2, 256, 512), BF),
            pltpu.VMEM((2, 256, 256), BF),
            pltpu.VMEM((128, 8, 128), BF),
            pltpu.VMEM((128, 8, 128), BF),
            pltpu.VMEM((128, 16, 128), BF),
            pltpu.VMEM((128, 16, 128), BF),
            pltpu.VMEM((2, 256, 512), BF),
            pltpu.VMEM((256, 8, 128), BF),
            pltpu.VMEM((2, 128, 8, 128), BF),
            pltpu.VMEM((128, 1024), F32),
            pltpu.SemaphoreType.DMA((2,)),
            pltpu.SemaphoreType.DMA((2,)),
        ]
        + [pltpu.SemaphoreType.DMA] * 8
        + [
            pltpu.SemaphoreType.DMA((6,)),
        ],
        compiler_params=pltpu.CompilerParams(
            collective_id=0, has_side_effects=True, vmem_limit_bytes=40 * 1024 * 1024
        ),
        name="triangles",
    )(pair_map, pair_mask, edge_weights, gate_weights, out_weights, norm_gains)


def solution(mesh):
    return jax.shard_map(
        per_device,
        mesh=mesh,
        in_specs=(P(("dap", "grp"), None, None), P(("dap", "grp"), None), P(), P(), P(), P()),
        out_specs=P(("dap", "grp"), None, None),
        check_vma=False,
    )
```

```python
import functools

import jax
import jax.numpy as jnp
from jax import lax
from jax.experimental import pallas as pl
from jax.experimental.pallas import tpu as pltpu
from jax.sharding import PartitionSpec as P

BF = jnp.bfloat16
F32 = jnp.float32
MESH = pl.DeviceIdType.MESH


def dot(a, b, ca, cb):
    return lax.dot_general(a, b, (((ca,), (cb,)), ((), ())), preferred_element_type=F32)


def one_hot(source):
    rows = lax.broadcasted_iota(jnp.int32, (256, 256), 0)
    cols = lax.broadcasted_iota(jnp.int32, (256, 256), 1)
    return jnp.where(cols == source(rows), 1.0, 0.0).astype(BF)


def ring(mask):
    return (0, 1, 2, 1)[mask]


XY_MASKS = sorted(((x, y) for x in range(4) for y in range(4)), key=lambda m: -ring(m[0]) - ring(m[1]))


def mesh_id(number):
    return (number >> 2, number & 3)


def kernel(z_hbm, mask_hbm, we_hbm, wg_hbm, wo_hbm, gains_hbm, out_ref,
           z_ref, mask_ref, we_ref, wg_ref, wo_ref, gains_ref, wt, perms, normed, cur, edges, send1, recvl, recvr, left, right, prod, send2, recv2,
           send3, recv3, pairs, send4, recv4, chan, sl, rl, sr, rr, s2, r2, s3, r3, s4, r4, load):
    dap = lax.axis_index("dap")
    number = dap * 4 + lax.axis_index("grp")
    core = (number >> 2) & 1
    z = ((number & 3) << 1) | (number >> 7)
    plane = number & (15 << 3)
    mine = ((number >> 2) << 1) | (number & 1)

    loads = [
        pltpu.make_async_copy(src, dst, load.at[i])
        for i, (src, dst) in enumerate(
            ((z_hbm, z_ref), (we_hbm, we_ref), (gains_hbm, gains_ref), (mask_hbm, mask_ref),
             (wg_hbm, wg_ref), (wo_hbm, wo_ref))
        )
    ]
    for copy in loads:
        copy.start()

    barrier = pltpu.get_barrier_semaphore()

    def everyone(visit):
        def one(k, carry):
            i = k >> 1
            at = (z + 4 + jnp.where((i & 1) == 1, 7 - (i >> 1), i >> 1)) & 7
            base = ((at & 1) << 7) | plane | (((k & 1) ^ core) << 2) | (at >> 1)
            for mx, my in XY_MASKS:
                visit(base ^ (my << 5 | mx << 3), mx == 0 and my == 0)
            return carry

        lax.fori_loop(0, 16, one, 0)

    def neighbours(visit, workers):
        def one(k, carry):
            i = k >> 1
            far = 2 + 4 * ((k & 1) if workers else 1 - core)
            at = (z + jnp.where(i == 0, far, jnp.where(i == 1, 1, jnp.where(i == 2, 7, 0)))) & 7
            base = ((at & 1) << 7) | plane | ((k & 1) << 2) | (at >> 1)
            for mx, my in XY_MASKS:
                visit(base ^ (my << 5 | mx << 3), mx == 0 and my == 0)
            return carry

        lax.fori_loop(0, 8, one, 0)

    def short(other):
        return ((other >> 2) << 1) | (other & 1)

    def sender(place, send_sem, recv_sem):
        def send(other, maybe_self):
            src, dst = place(other)
            copy = pltpu.make_async_remote_copy(
                src_ref=src, dst_ref=dst, send_sem=send_sem, recv_sem=recv_sem, device_id=mesh_id(other),
                device_id_type=MESH,
            )
            if not maybe_self:
                copy.start()
                return
            pl.when(other != number)(copy.start)

            @pl.when(other == number)
            def _():
                pltpu.make_async_copy(src, dst, recv_sem).start()

        return send

    def greet(other, maybe_self):
        def signal():
            pl.semaphore_signal(barrier, inc=1, device_id=mesh_id(other), device_id_type=MESH)

        if maybe_self:
            pl.when(other != number)(signal)
        else:
            signal()

    everyone(greet)

    perms[0] = one_hot(lambda r: (r % 8) * 32 + r // 8)
    perms[1] = one_hot(lambda r: ((r // 2) % 32) * 8 + (r % 2) * 4 + r // 64)
    perms[4] = one_hot(lambda r: (r % 16) * 16 + r // 16)
    perms[5] = one_hot(lambda r: ((r // 2) % 16) * 16 + (r // 128) * 8 + (r % 2) * 4 + (r // 32) % 4)
    perms[2] = one_hot(lambda r: (r % 4) * 64 + r // 4)
    perms[3] = one_hot(lambda r: (r % 32) * 8 + r // 32)

    for copy in loads:
        copy.wait()
    for u in range(2):
        wt[u] = we_ref[u].astype(F32).T.astype(BF)

    def normalize_rows(u, source):
        gain = gains_ref[u, 0:1, :]
        for p in range(4):
            row, lanes = p // 2, slice(p % 2 * 256, p % 2 * 256 + 256)
            zf = source[row, lanes, :].astype(F32)
            centred = zf - jnp.mean(zf, axis=1, keepdims=True)
            variance = jnp.mean(centred * centred, axis=1, keepdims=True)
            normed[u, row, lanes, :] = (centred * lax.rsqrt(variance + 1e-05) * gain).astype(BF)

    def edge_map(u, lr):
        for p in range(4):
            row, lanes = p // 2, slice(p % 2 * 256, p % 2 * 256 + 256)
            mask = mask_ref[row : row + 1, lanes].astype(F32)
            proj = dot(wt[u, lr * 256 : lr * 256 + 256, :], normed[u, row, lanes, :], 1, 1)
            edge = jax.nn.sigmoid(proj[:128]) * proj[128:] * mask
            edges[lr, :, p * 256 : p * 256 + 256] = edge.astype(BF)

    def pack_one(lr):
        for b in range(4):
            rows = slice(b * 32, b * 32 + 32)
            stack = jnp.concatenate([edges[lr, rows, j * 128 : j * 128 + 128] for j in range(8)], axis=0)
            send1[lr, rows] = dot(perms[0], stack, 1, 0).reshape(32, 8, 128).astype(BF)

    def pack_both():
        for b in range(8):
            rows = slice(b * 16, b * 16 + 16)
            stack = jnp.concatenate(
                [edges[lr, rows, j * 128 : j * 128 + 128] for lr in range(2) for j in range(8)], axis=0
            )
            send3[rows] = dot(perms[4], stack, 1, 0).astype(BF).reshape(16, 16, 128)

    def wait_all(buf, sem):
        pltpu.make_async_copy(buf, buf, sem).wait()

    def gathered(buf, b):
        wanted = buf[b * 32 : b * 32 + 32].astype(F32).reshape(256, 128).astype(BF)
        blocks = dot(perms[1], wanted, 1, 0).astype(BF)
        return [blocks[k * 64 : k * 64 + 64] for k in range(4)]

    def messages(rows_of):
        stack = jnp.concatenate(rows_of, axis=0)
        return dot(perms[2], stack, 1, 0).reshape(32, 8, 128).astype(BF)

    def multiply_outgoing():
        for sem, buf, edge, blocks in ((rr, recvr, right, 8), (rl, recvl, left, 4)):
            wait_all(buf, sem)
            for b in range(blocks):
                for k, block in enumerate(gathered(buf, b)):
                    edge[b * 64 : b * 64 + 64, k * 128 : k * 128 + 128] = block
        for half in range(2):
            prod[half] = dot(left[...], right[half * 256 : half * 256 + 256], 1, 1).astype(BF)
        for b in range(4):
            rows = slice(b * 64, b * 64 + 64)
            send2[b * 32 : b * 32 + 32] = messages(
                [prod[j // 2, rows, (j % 2) * 128 : (j % 2) * 128 + 128] for j in range(4)]
            )

    def multiply_incoming():
        wait_all(recv3, r3)
        for b in range(8):
            wanted = recv3[b * 16 : b * 16 + 16].reshape(256, 128)
            blocks = dot(perms[5], wanted, 1, 0).astype(BF)
            for lr in range(2):
                for k in range(4):
                    pairs[lr, b * 32 : b * 32 + 32, k * 128 : k * 128 + 128] = blocks[
                        lr * 128 + k * 32 : lr * 128 + k * 32 + 32
                    ]
        for i in range(2):
            part = dot(pairs[0, :, i * 256 : i * 256 + 256], pairs[1], 0, 0).astype(BF)
            for b in range(4):
                send4[i * 128 + b * 32 : i * 128 + b * 32 + 32] = messages(
                    [part[b * 64 : b * 64 + 64, j * 128 : j * 128 + 128] for j in range(4)]
                )

    def by_channel(buf, b):
        block = buf[b * 32 : b * 32 + 32].astype(F32).reshape(256, 128).astype(BF)
        return dot(perms[3], block, 1, 0)

    def finish(u, source, target):
        if u == 0:
            wait_all(recv2, r2)
        else:
            wait_all(recv4, r4)
        for b in range(4):
            if u == 0:
                tiles = by_channel(recv2, b)
            else:
                tiles = by_channel(recv4.at[0], b) + by_channel(recv4.at[1], b)
            for j in range(8):
                chan[b * 32 : b * 32 + 32, j * 128 : j * 128 + 128] = tiles[j * 32 : j * 32 + 32]
        gain = gains_ref[u, 1:2, :].reshape(128, 1)
        for p in range(4):
            row, half = p // 2, p % 2
            lanes = slice(half * 256, half * 256 + 256)
            values = chan[:, p * 256 : p * 256 + 256]
            centred = values - jnp.mean(values, axis=0, keepdims=True)
            variance = jnp.mean(centred * centred, axis=0, keepdims=True)
            scaled = (centred * lax.rsqrt(variance + 1e-05) * gain).astype(BF)
            projected = dot(scaled, wo_ref[u], 0, 0)
            gating = jax.nn.sigmoid(dot(normed[u, row, lanes, :], wg_ref[u], 1, 0))
            result = source[row, lanes, :].astype(F32) + gating * projected
            target[row, lanes, :] = result.astype(BF)

    normalize_rows(0, z_ref)
    for lr in (1, 0):
        edge_map(0, lr)
        pack_one(lr)
    pl.semaphore_wait(barrier, 255)
    everyone(sender(lambda other: (send1.at[1, short(other)], recvr.at[number]), sr, rr))
    neighbours(sender(lambda other: (send1.at[0, short(other)], recvl.at[mine]), sl, rl), True)
    multiply_outgoing()
    neighbours(sender(lambda other: (send2.at[short(other)], recv2.at[mine]), s2, r2), False)
    finish(0, z_ref, cur)

    normalize_rows(1, cur)
    edge_map(1, 0)
    edge_map(1, 1)
    pack_both()
    neighbours(sender(lambda other: (send3.at[short(other)], recv3.at[mine]), s3, r3), True)
    multiply_incoming()
    part = (number >> 1) & 1
    everyone(sender(lambda other: (send4.at[other], recv4.at[part, mine]), s4, r4))
    finish(1, cur, out_ref)

    wait_all(send4.at[pl.ds(0, 255)], sr)
    wait_all(send1.at[0, pl.ds(0, 127)], sl)
    wait_all(send2.at[pl.ds(0, 127)], s2)
    wait_all(send3.at[pl.ds(0, 127)], s3)
    wait_all(send4.at[pl.ds(0, 255)], s4)


def per_device(pair_map, pair_mask, edge_weights, gate_weights, out_weights, norm_gains):
    vmem = pl.BlockSpec(memory_space=pltpu.VMEM)
    return pl.pallas_call(
        kernel,
        out_shape=jax.ShapeDtypeStruct((2, 512, 128), BF),
        in_specs=[pl.BlockSpec(memory_space=pl.ANY)] * 6,
        out_specs=vmem,
        scratch_shapes=[
            pltpu.VMEM((2, 512, 128), BF),
            pltpu.VMEM((2, 512), jnp.int32),
            pltpu.VMEM((2, 128, 512), BF),
            pltpu.VMEM((2, 128, 128), BF),
            pltpu.VMEM((2, 128, 128), BF),
            pltpu.VMEM((2, 2, 128), F32),
            pltpu.VMEM((2, 512, 128), BF),
            pltpu.VMEM((6, 256, 256), BF),
            pltpu.VMEM((2, 2, 512, 128), BF),
            pltpu.VMEM((2, 512, 128), BF),
            pltpu.VMEM((2, 128, 1024), BF),
            pltpu.VMEM((2, 128, 8, 128), BF),
            pltpu.VMEM((128, 8, 128), BF),
            pltpu.VMEM((256, 8, 128), BF),
            pltpu.VMEM((256, 512), BF),
            pltpu.VMEM((512, 512), BF),
            pltpu.VMEM((2, 256, 256), BF),
            pltpu.VMEM((128, 8, 128), BF),
            pltpu.VMEM((128, 8, 128), BF),
            pltpu.VMEM((128, 16, 128), BF),
            pltpu.VMEM((128, 16, 128), BF),
            pltpu.VMEM((2, 256, 512), BF),
            pltpu.VMEM((256, 8, 128), BF),
            pltpu.VMEM((2, 128, 8, 128), BF),
            pltpu.VMEM((128, 1024), F32),
        ]
        + [pltpu.SemaphoreType.DMA] * 10
        + [
            pltpu.SemaphoreType.DMA((6,)),
        ],
        compiler_params=pltpu.CompilerParams(
            collective_id=0, has_side_effects=True, vmem_limit_bytes=40 * 1024 * 1024
        ),
        name="triangles",
    )(pair_map, pair_mask, edge_weights, gate_weights, out_weights, norm_gains)


def solution(mesh):
    return jax.shard_map(
        per_device,
        mesh=mesh,
        in_specs=(P(("dap", "grp"), None, None), P(("dap", "grp"), None), P(), P(), P(), P()),
        out_specs=P(("dap", "grp"), None, None),
        check_vma=False,
    )
```

```python
import functools

import jax
import jax.numpy as jnp
from jax import lax
from jax.experimental import pallas as pl
from jax.experimental.pallas import tpu as pltpu
from jax.sharding import PartitionSpec as P

BF = jnp.bfloat16
F32 = jnp.float32
MESH = pl.DeviceIdType.MESH


def dot(a, b, ca, cb):
    return lax.dot_general(a, b, (((ca,), (cb,)), ((), ())), preferred_element_type=F32)


def one_hot(source):
    rows = lax.broadcasted_iota(jnp.int32, (256, 256), 0)
    cols = lax.broadcasted_iota(jnp.int32, (256, 256), 1)
    return jnp.where(cols == source(rows), 1.0, 0.0).astype(BF)


def ring(mask):
    return (0, 1, 2, 1)[mask]


XY_MASKS = sorted(((x, y) for x in range(4) for y in range(4)), key=lambda m: -ring(m[0]) - ring(m[1]))
Z_MASKS = (4, 5, 7, 3, 2, 6, 1, 0)
Z_EVEN = (4, 2, 6, 0)
Z_ODD = (5, 7, 3, 1)


def packed(masks):
    return sum((((m & 1) << 3) | (m >> 1)) << (4 * i) for i, m in enumerate(masks) if i < 7)


def nibble(word, i):
    return (word >> (4 * i)) & 15


def mesh_id(number):
    return (number >> 2, number & 3)


def kernel(z_hbm, mask_hbm, we_hbm, wg_hbm, wo_hbm, gains_hbm, out_hbm,
           z_ref, mask_ref, we_ref, wg_ref, wo_ref, gains_ref, wt, perms, normed, cur, edges, send1, recv1, left, right, send2, recv2,
           send3, recv3, pairs, send4, recv4, chan, result, s1, r1, s2, r2, s3, r3, s4, r4, sx, rx, load, store):
    dap = lax.axis_index("dap")
    number = dap * 4 + lax.axis_index("grp")
    core = (number >> 2) & 1
    zlo = number >> 7
    slot = number & 127
    channel = ((number >> 3) << 2) | (number & 3)
    sibling = mesh_id(number ^ 4)

    loads = [
        pltpu.make_async_copy(src, dst, load.at[i])
        for i, (src, dst) in enumerate(
            ((z_hbm, z_ref), (we_hbm, we_ref), (gains_hbm, gains_ref), (mask_hbm, mask_ref),
             (wg_hbm, wg_ref), (wo_hbm, wo_ref))
        )
    ]
    for copy in loads:
        copy.start()

    barrier = pltpu.get_barrier_semaphore()

    def partners(visit, masks=XY_MASKS):
        word = jnp.where(zlo == core, packed(Z_EVEN), packed(Z_ODD))
        chip = number - core * 4

        def one(k, carry):
            z = nibble(word, k & 3)
            base = chip ^ (((z >> 3) << 7) | (z & 3) | ((k >> 2) << 2))
            for mx, my in masks:
                visit(base ^ (my << 5 | mx << 3))
            return carry

        lax.fori_loop(0, 8, one, 0)

    def greet(other):
        @pl.when((other | 4) != (number | 4))
        def _():
            pl.semaphore_signal(barrier, inc=1, device_id=mesh_id(other), device_id_type=MESH)

    pl.semaphore_signal(barrier, inc=1, device_id=sibling, device_id_type=MESH)
    partners(greet)

    perms[0] = one_hot(lambda r: (r % 8) * 32 + r // 8)
    perms[1] = one_hot(lambda r: ((r // 2) % 32) * 8 + (r % 2) * 4 + r // 64)
    perms[4] = one_hot(lambda r: (r % 16) * 16 + r // 16)
    perms[5] = one_hot(lambda r: ((r // 2) % 16) * 16 + (r // 128) * 8 + (r % 2) * 4 + (r // 32) % 4)
    perms[2] = one_hot(lambda r: (r % 4) * 64 + r // 4)
    perms[3] = one_hot(lambda r: (r % 32) * 8 + r // 32)

    for copy in loads:
        copy.wait()
    for u in range(2):
        wt[u] = we_ref[u].astype(F32).T.astype(BF)

    def normalize_rows(u, source):
        gain = gains_ref[u, 0:1, :]
        for p in range(4):
            row, lanes = p // 2, slice(p % 2 * 256, p % 2 * 256 + 256)
            zf = source[row, lanes, :].astype(F32)
            centred = zf - jnp.mean(zf, axis=1, keepdims=True)
            variance = jnp.mean(centred * centred, axis=1, keepdims=True)
            normed[u, row, lanes, :] = (centred * lax.rsqrt(variance + 1e-05) * gain).astype(BF)

    def edge_map(u, lr):
        for p in range(4):
            row, lanes = p // 2, slice(p % 2 * 256, p % 2 * 256 + 256)
            mask = mask_ref[row : row + 1, lanes].astype(F32)
            proj = dot(wt[u, lr * 256 : lr * 256 + 256, :], normed[u, row, lanes, :], 1, 1)
            edge = jax.nn.sigmoid(proj[:128]) * proj[128:] * mask
            edges[lr, :, p * 256 : p * 256 + 256] = edge.astype(BF)

    def pack_one(lr):
        for b in range(4):
            rows = slice(b * 32, b * 32 + 32)
            stack = jnp.concatenate([edges[lr, rows, j * 128 : j * 128 + 128] for j in range(8)], axis=0)
            send1[lr, rows] = dot(perms[0], stack, 1, 0).reshape(32, 8, 128).astype(BF)

    def edges_of(base):
        for p in range(4):
            row, lanes = p // 2, slice(p % 2 * 256, p % 2 * 256 + 256)
            mask = mask_ref[row : row + 1, lanes].astype(F32)
            for lr in range(2):
                gate = dot(wt[1, pl.ds(base + lr * 256, 64), :], normed[1, row, lanes, :], 1, 1)
                value = dot(wt[1, pl.ds(base + lr * 256 + 128, 64), :], normed[1, row, lanes, :], 1, 1)
                edges[lr, 0:64, p * 256 : p * 256 + 256] = (jax.nn.sigmoid(gate) * value * mask).astype(BF)
        for b in range(4):
            rows = slice(b * 16, b * 16 + 16)
            stack = jnp.concatenate(
                [edges[lr, rows, j * 128 : j * 128 + 128] for lr in range(2) for j in range(8)], axis=0
            )
            send3[pl.ds(base + b * 16, 16)] = dot(perms[4], stack, 1, 0).astype(BF).reshape(16, 16, 128)

    def scatter_edges(lr):
        base = (number - core * 4) | (zlo << 2)

        def one(k, carry):
            z = jnp.where(k == 7, 0, nibble(packed(Z_MASKS), k))
            for mx, my in XY_MASKS:
                other = base ^ (((z >> 3) << 7) | (z & 3) | (my << 5 | mx << 3))
                h = channel ^ (((z >> 3) << 6) | (z & 3) | (my << 4 | mx << 2))
                copy = pltpu.make_async_remote_copy(
                    src_ref=send1.at[lr, h], dst_ref=recv1.at[lr, slot], send_sem=s1.at[lr],
                    recv_sem=r1.at[lr],
                    device_id=mesh_id(other), device_id_type=MESH,
                )
                if mx or my:
                    copy.start()
                    continue
                pl.when(other != number)(copy.start)

                @pl.when(other == number)
                def _():
                    pltpu.make_async_copy(send1.at[lr, h], recv1.at[lr, slot], r1.at[lr]).start()

            return carry

        lax.fori_loop(0, 8, one, 0)

    def scatter_products(masks):
        def send(other):
            at = other & 127

            @pl.when(other != number)
            def _():
                pltpu.make_async_remote_copy(
                    src_ref=send2.at[at], dst_ref=recv2.at[channel], send_sem=s2, recv_sem=r2,
                    device_id=mesh_id(other), device_id_type=MESH,
                ).start()

            @pl.when(other == number)
            def _():
                pltpu.make_async_copy(send2.at[at], recv2.at[channel], r2).start()

        partners(send, masks)

    mine = ((number >> 2) << 1) | (number & 1)

    def scatter_pairs(odd):
        z = ((number & 3) << 1) | zlo
        plane = number & (15 << 3)

        def one(k, carry):
            worker_core = k & 1
            step = k >> 1
            dz = jnp.where(step == 0, 1, 7) if odd else jnp.where(step == 0, 2 + 4 * worker_core, 0)
            wz = (z + dz) & 7
            base = ((wz & 1) << 7) | plane | (worker_core << 2) | (wz >> 1)
            for mx, my in XY_MASKS:
                other = base ^ (my << 5 | mx << 3)
                h = ((other >> 2) << 1) | (other & 1)
                copy = pltpu.make_async_remote_copy(
                    src_ref=send3.at[h], dst_ref=recv3.at[mine], send_sem=s3, recv_sem=r3,
                    device_id=mesh_id(other), device_id_type=MESH,
                )
                if mx or my:
                    copy.start()
                    continue
                pl.when(other != number)(copy.start)

                @pl.when(other == number)
                def _():
                    pltpu.make_async_copy(send3.at[h], recv3.at[mine], r3).start()

            return carry

        lax.fori_loop(0, 4, one, 0)

    def scatter_parts(masks):
        part = (number >> 1) & 1

        def one(k, carry):
            z = nibble(packed(masks), k >> 1)
            base = number ^ (((z >> 3) << 7) | (z & 3) | ((k & 1) << 2))
            for mx, my in XY_MASKS:
                other = base ^ (my << 5 | mx << 3)
                copy = pltpu.make_async_remote_copy(
                    src_ref=send4.at[other], dst_ref=recv4.at[part, mine], send_sem=s4, recv_sem=r4,
                    device_id=mesh_id(other), device_id_type=MESH,
                )
                if mx or my:
                    copy.start()
                    continue
                pl.when(other != number)(copy.start)

                @pl.when(other == number)
                def _():
                    pltpu.make_async_copy(send4.at[other], recv4.at[part, mine], r4).start()

            return carry

        lax.fori_loop(0, 8, one, 0)

    def wait_all(buf, sem):
        pltpu.make_async_copy(buf, buf, sem).wait()

    def gathered(lr, b):
        wanted = recv1[lr, b * 32 : b * 32 + 32].astype(F32).reshape(256, 128).astype(BF)
        blocks = dot(perms[1], wanted, 1, 0).astype(BF)
        return [blocks[k * 64 : k * 64 + 64] for k in range(4)]

    def messages(rows_of):
        stack = jnp.concatenate(rows_of, axis=0)
        return dot(perms[2], stack, 1, 0).reshape(32, 8, 128).astype(BF)

    def multiply_outgoing():
        wait_all(recv1.at[1], r1.at[1])
        for b in range(4):
            for k, block in enumerate(gathered(1, b)):
                right[core, b * 64 : b * 64 + 64, k * 128 : k * 128 + 128] = block
        relay = pltpu.make_async_remote_copy(
            src_ref=right.at[core], dst_ref=right.at[core], send_sem=sx, recv_sem=rx, device_id=sibling,
            device_id_type=MESH,
        )
        relay.start()
        wait_all(recv1.at[0], r1.at[0])
        for b in range(4):
            for k, block in enumerate(gathered(0, b)):
                left[b * 64 : b * 64 + 64, k * 128 : k * 128 + 128] = block
        relay.wait_recv()
        top = (number >> 6) & 1
        for flip in (1, 0):
            first = pl.multiple_of((top ^ flip) * 128, 128)
            rows = left[pl.ds(first, 128), :]
            halves = [dot(rows, right[j], 1, 1).astype(BF) for j in range(2)]
            for b in range(2):
                send2[pl.ds((top ^ flip) * 64 + b * 32, 32)] = messages(
                    [halves[j // 2][b * 64 : b * 64 + 64, (j % 2) * 128 : (j % 2) * 128 + 128] for j in range(4)]
                )
            scatter_products([m for m in XY_MASKS if m[1] >> 1 == flip])
        return relay

    def multiply_incoming():
        wait_all(recv3, r3)
        for b in range(8):
            wanted = recv3[b * 16 : b * 16 + 16].reshape(256, 128)
            blocks = dot(perms[5], wanted, 1, 0).astype(BF)
            for lr in range(2):
                for k in range(4):
                    pairs[lr, b * 32 : b * 32 + 32, k * 128 : k * 128 + 128] = blocks[
                        lr * 128 + k * 32 : lr * 128 + k * 32 + 32
                    ]
        for masks, flip in ((Z_EVEN, 0), (Z_ODD, 1)):
            half = zlo ^ flip
            lhs = pairs[0, :, pl.ds(pl.multiple_of(half * 256, 256), 256)]
            part = dot(lhs, pairs[1], 0, 0).astype(BF)
            for b in range(4):
                send4[pl.ds(half * 128 + b * 32, 32)] = messages(
                    [part[b * 64 : b * 64 + 64, j * 128 : j * 128 + 128] for j in range(4)]
                )
            scatter_parts(masks)

    def by_channel(buf, b):
        block = buf[b * 32 : b * 32 + 32].astype(F32).reshape(256, 128).astype(BF)
        return dot(perms[3], block, 1, 0)

    def finish(u, source, target):
        if u == 0:
            wait_all(recv2, r2)
        else:
            wait_all(recv4, r4)
        for b in range(4):
            if u == 0:
                tiles = by_channel(recv2, b)
            else:
                tiles = by_channel(recv4.at[0], b) + by_channel(recv4.at[1], b)
            for j in range(8):
                chan[b * 32 : b * 32 + 32, j * 128 : j * 128 + 128] = tiles[j * 32 : j * 32 + 32]
        gain = gains_ref[u, 1:2, :].reshape(128, 1)
        for p in range(4):
            row, half = p // 2, p % 2
            lanes = slice(half * 256, half * 256 + 256)
            values = chan[:, p * 256 : p * 256 + 256]
            centred = values - jnp.mean(values, axis=0, keepdims=True)
            variance = jnp.mean(centred * centred, axis=0, keepdims=True)
            scaled = (centred * lax.rsqrt(variance + 1e-05) * gain).astype(BF)
            projected = dot(scaled, wo_ref[u], 0, 0)
            gating = jax.nn.sigmoid(dot(normed[u, row, lanes, :], wg_ref[u], 1, 0))
            updated = source[row, lanes, :].astype(F32) + gating * projected
            target[row, lanes, :] = updated.astype(BF)
            if u == 1:
                stores.append(pltpu.make_async_copy(target.at[row, lanes], out_hbm.at[row, lanes], store.at[p]))
                stores[-1].start()

    stores = []
    normalize_rows(0, z_ref)
    for lr in (1, 0):
        edge_map(0, lr)
        pack_one(lr)
    pl.semaphore_wait(barrier, 128)
    scatter_edges(1)
    scatter_edges(0)
    relay = multiply_outgoing()
    finish(0, z_ref, cur)

    normalize_rows(1, cur)
    edges_of(pl.multiple_of(zlo * 64, 64))
    scatter_pairs(False)
    edges_of(pl.multiple_of((1 - zlo) * 64, 64))
    scatter_pairs(True)
    multiply_incoming()
    finish(1, cur, result)

    for copy in stores:
        copy.wait()
    relay.wait_send()
    wait_all(send3.at[pl.ds(0, 127)], s3)
    wait_all(send4.at[pl.ds(0, 255)], s4)

    @pl.when(zlo == core)
    def _():
        for lr in range(2):
            wait_all(send1.at[lr, pl.ds(0, 127)], s1.at[lr])
        wait_all(send2.at[pl.ds(0, 127)], s2)

    @pl.when(zlo != core)
    def _():
        for lr in range(2):
            wait_all(send1.at[lr], s1.at[lr])
        wait_all(send2, s2)


def per_device(pair_map, pair_mask, edge_weights, gate_weights, out_weights, norm_gains):
    return pl.pallas_call(
        kernel,
        out_shape=jax.ShapeDtypeStruct((2, 512, 128), BF),
        in_specs=[pl.BlockSpec(memory_space=pl.ANY)] * 6,
        out_specs=pl.BlockSpec(memory_space=pl.ANY),
        scratch_shapes=[
            pltpu.VMEM((2, 512, 128), BF),
            pltpu.VMEM((2, 512), jnp.int32),
            pltpu.VMEM((2, 128, 512), BF),
            pltpu.VMEM((2, 128, 128), BF),
            pltpu.VMEM((2, 128, 128), BF),
            pltpu.VMEM((2, 2, 128), F32),
            pltpu.VMEM((2, 512, 128), BF),
            pltpu.VMEM((6, 256, 256), BF),
            pltpu.VMEM((2, 2, 512, 128), BF),
            pltpu.VMEM((2, 512, 128), BF),
            pltpu.VMEM((2, 128, 1024), BF),
            pltpu.VMEM((2, 128, 8, 128), BF),
            pltpu.VMEM((2, 128, 8, 128), BF),
            pltpu.VMEM((256, 512), BF),
            pltpu.VMEM((2, 256, 512), BF),
            pltpu.VMEM((128, 8, 128), BF),
            pltpu.VMEM((128, 8, 128), BF),
            pltpu.VMEM((128, 16, 128), BF),
            pltpu.VMEM((128, 16, 128), BF),
            pltpu.VMEM((2, 256, 512), BF),
            pltpu.VMEM((256, 8, 128), BF),
            pltpu.VMEM((2, 128, 8, 128), BF),
            pltpu.VMEM((128, 1024), F32),
            pltpu.VMEM((2, 512, 128), BF),
            pltpu.SemaphoreType.DMA((2,)),
            pltpu.SemaphoreType.DMA((2,)),
        ]
        + [pltpu.SemaphoreType.DMA] * 8
        + [
            pltpu.SemaphoreType.DMA((6,)),
            pltpu.SemaphoreType.DMA((4,)),
        ],
        compiler_params=pltpu.CompilerParams(
            collective_id=0, has_side_effects=True, vmem_limit_bytes=40 * 1024 * 1024
        ),
        name="triangles",
    )(pair_map, pair_mask, edge_weights, gate_weights, out_weights, norm_gains)


def solution(mesh):
    return jax.shard_map(
        per_device,
        mesh=mesh,
        in_specs=(P(("dap", "grp"), None, None), P(("dap", "grp"), None), P(), P(), P(), P()),
        out_specs=P(("dap", "grp"), None, None),
        check_vma=False,
    )
```

```python
import functools

import jax
import jax.numpy as jnp
from jax import lax
from jax.experimental import pallas as pl
from jax.experimental.pallas import tpu as pltpu
from jax.sharding import PartitionSpec as P

BF = jnp.bfloat16
F32 = jnp.float32
MESH = pl.DeviceIdType.MESH


def dot(a, b, ca, cb):
    return lax.dot_general(a, b, (((ca,), (cb,)), ((), ())), preferred_element_type=F32)


def one_hot(source):
    rows = lax.broadcasted_iota(jnp.int32, (256, 256), 0)
    cols = lax.broadcasted_iota(jnp.int32, (256, 256), 1)
    return jnp.where(cols == source(rows), 1.0, 0.0).astype(BF)


def ring(mask):
    return (0, 1, 2, 1)[mask]


XY_MASKS = sorted(((x, y) for x in range(4) for y in range(4)), key=lambda m: -ring(m[0]) - ring(m[1]))
Z_MASKS = (4, 5, 7, 3, 2, 6, 1, 0)
Z_EVEN = (4, 2, 6, 0)
Z_ODD = (5, 7, 3, 1)


def packed(masks):
    return sum((((m & 1) << 3) | (m >> 1)) << (4 * i) for i, m in enumerate(masks) if i < 7)


def nibble(word, i):
    return (word >> (4 * i)) & 15


def mesh_id(number):
    return (number >> 2, number & 3)


def kernel(z_hbm, mask_hbm, we_hbm, wg_hbm, wo_hbm, gains_hbm, out_ref,
           z_ref, mask_ref, we_ref, wg_ref, wo_ref, gains_ref, wt, perms, normed, cur, edges, send1, recv1, left, right, send2, recv2,
           send3, recv3, pairs, send4, recv4, chan, s1, r1, s2, r2, s3, r3, s4, r4, sx, rx, load):
    dap = lax.axis_index("dap")
    number = dap * 4 + lax.axis_index("grp")
    core = (number >> 2) & 1
    zlo = number >> 7
    slot = number & 127
    channel = ((number >> 3) << 2) | (number & 3)
    sibling = mesh_id(number ^ 4)

    loads = [
        pltpu.make_async_copy(src, dst, load.at[i])
        for i, (src, dst) in enumerate(
            ((z_hbm, z_ref), (we_hbm, we_ref), (gains_hbm, gains_ref), (mask_hbm, mask_ref),
             (wg_hbm, wg_ref), (wo_hbm, wo_ref))
        )
    ]
    for copy in loads:
        copy.start()

    barrier = pltpu.get_barrier_semaphore()

    def partners(visit, masks=XY_MASKS):
        word = jnp.where(zlo == core, packed(Z_EVEN), packed(Z_ODD))
        chip = number - core * 4

        def one(k, carry):
            z = nibble(word, k & 3)
            base = chip ^ (((z >> 3) << 7) | (z & 3) | ((k >> 2) << 2))
            for mx, my in masks:
                visit(base ^ (my << 5 | mx << 3))
            return carry

        lax.fori_loop(0, 8, one, 0)

    def greet(other):
        @pl.when((other | 4) != (number | 4))
        def _():
            pl.semaphore_signal(barrier, inc=1, device_id=mesh_id(other), device_id_type=MESH)

    pl.semaphore_signal(barrier, inc=1, device_id=sibling, device_id_type=MESH)
    partners(greet)

    perms[0] = one_hot(lambda r: (r % 8) * 32 + r // 8)
    perms[1] = one_hot(lambda r: ((r // 2) % 32) * 8 + (r % 2) * 4 + r // 64)
    perms[4] = one_hot(lambda r: (r % 16) * 16 + r // 16)
    perms[5] = one_hot(lambda r: ((r // 2) % 16) * 16 + (r // 128) * 8 + (r % 2) * 4 + (r // 32) % 4)
    perms[2] = one_hot(lambda r: (r % 4) * 64 + r // 4)
    perms[3] = one_hot(lambda r: (r % 32) * 8 + r // 32)

    for copy in loads:
        copy.wait()
    for u in range(2):
        wt[u] = we_ref[u].astype(F32).T.astype(BF)

    def normalize_rows(u, source):
        gain = gains_ref[u, 0:1, :]
        for p in range(4):
            row, lanes = p // 2, slice(p % 2 * 256, p % 2 * 256 + 256)
            zf = source[row, lanes, :].astype(F32)
            centred = zf - jnp.mean(zf, axis=1, keepdims=True)
            variance = jnp.mean(centred * centred, axis=1, keepdims=True)
            normed[u, row, lanes, :] = (centred * lax.rsqrt(variance + 1e-05) * gain).astype(BF)

    def edge_map(u, lr):
        for p in range(4):
            row, lanes = p // 2, slice(p % 2 * 256, p % 2 * 256 + 256)
            mask = mask_ref[row : row + 1, lanes].astype(F32)
            proj = dot(wt[u, lr * 256 : lr * 256 + 256, :], normed[u, row, lanes, :], 1, 1)
            edge = jax.nn.sigmoid(proj[:128]) * proj[128:] * mask
            edges[lr, :, p * 256 : p * 256 + 256] = edge.astype(BF)

    def pack_one(lr):
        for b in range(4):
            rows = slice(b * 32, b * 32 + 32)
            stack = jnp.concatenate([edges[lr, rows, j * 128 : j * 128 + 128] for j in range(8)], axis=0)
            send1[lr, rows] = dot(perms[0], stack, 1, 0).reshape(32, 8, 128).astype(BF)

    def edges_of(base):
        weights = jnp.concatenate([wt[1, pl.ds(base + c * 128, 64), :] for c in range(4)], axis=0)
        for p in range(4):
            row, lanes = p // 2, slice(p % 2 * 256, p % 2 * 256 + 256)
            mask = mask_ref[row : row + 1, lanes].astype(F32)
            proj = dot(weights, normed[1, row, lanes, :], 1, 1)
            for lr in range(2):
                gate, value = proj[lr * 128 : lr * 128 + 64], proj[lr * 128 + 64 : lr * 128 + 128]
                edges[lr, 0:64, p * 256 : p * 256 + 256] = (jax.nn.sigmoid(gate) * value * mask).astype(BF)
        for b in range(4):
            rows = slice(b * 16, b * 16 + 16)
            stack = jnp.concatenate(
                [edges[lr, rows, j * 128 : j * 128 + 128] for lr in range(2) for j in range(8)], axis=0
            )
            send3[pl.ds(base + b * 16, 16)] = dot(perms[4], stack, 1, 0).astype(BF).reshape(16, 16, 128)

    def scatter_edges(lr):
        base = (number - core * 4) | (zlo << 2)

        def one(k, carry):
            z = jnp.where(k == 7, 0, nibble(packed(Z_MASKS), k))
            for mx, my in XY_MASKS:
                other = base ^ (((z >> 3) << 7) | (z & 3) | (my << 5 | mx << 3))
                h = channel ^ (((z >> 3) << 6) | (z & 3) | (my << 4 | mx << 2))
                copy = pltpu.make_async_remote_copy(
                    src_ref=send1.at[lr, h], dst_ref=recv1.at[lr, slot], send_sem=s1.at[lr],
                    recv_sem=r1.at[lr],
                    device_id=mesh_id(other), device_id_type=MESH,
                )
                if mx or my:
                    copy.start()
                    continue
                pl.when(other != number)(copy.start)

                @pl.when(other == number)
                def _():
                    pltpu.make_async_copy(send1.at[lr, h], recv1.at[lr, slot], r1.at[lr]).start()

            return carry

        lax.fori_loop(0, 8, one, 0)

    def scatter_products(masks):
        def send(other):
            at = other & 127

            @pl.when(other != number)
            def _():
                pltpu.make_async_remote_copy(
                    src_ref=send2.at[at], dst_ref=recv2.at[channel], send_sem=s2, recv_sem=r2,
                    device_id=mesh_id(other), device_id_type=MESH,
                ).start()

            @pl.when(other == number)
            def _():
                pltpu.make_async_copy(send2.at[at], recv2.at[channel], r2).start()

        partners(send, masks)

    mine = ((number >> 2) << 1) | (number & 1)

    def scatter_pairs(odd):
        z = ((number & 3) << 1) | zlo
        plane = number & (15 << 3)

        def one(k, carry):
            worker_core = k & 1
            step = k >> 1
            dz = jnp.where(step == 0, 1, 7) if odd else jnp.where(step == 0, 2 + 4 * worker_core, 0)
            wz = (z + dz) & 7
            base = ((wz & 1) << 7) | plane | (worker_core << 2) | (wz >> 1)
            for mx, my in XY_MASKS:
                other = base ^ (my << 5 | mx << 3)
                h = ((other >> 2) << 1) | (other & 1)
                copy = pltpu.make_async_remote_copy(
                    src_ref=send3.at[h], dst_ref=recv3.at[mine], send_sem=s3, recv_sem=r3,
                    device_id=mesh_id(other), device_id_type=MESH,
                )
                if mx or my:
                    copy.start()
                    continue
                pl.when(other != number)(copy.start)

                @pl.when(other == number)
                def _():
                    pltpu.make_async_copy(send3.at[h], recv3.at[mine], r3).start()

            return carry

        lax.fori_loop(0, 4, one, 0)

    def scatter_parts(masks):
        part = (number >> 1) & 1

        def one(k, carry):
            zk = k >> 1
            z = jnp.where(zk == 7, 0, nibble(packed(Z_MASKS), zk))
            base = number ^ (((z >> 3) << 7) | (z & 3) | ((k & 1) << 2))
            for mx, my in masks:
                other = base ^ (my << 5 | mx << 3)
                copy = pltpu.make_async_remote_copy(
                    src_ref=send4.at[other], dst_ref=recv4.at[part, mine], send_sem=s4, recv_sem=r4,
                    device_id=mesh_id(other), device_id_type=MESH,
                )
                if mx or my:
                    copy.start()
                    continue
                pl.when(other != number)(copy.start)

                @pl.when(other == number)
                def _():
                    pltpu.make_async_copy(send4.at[other], recv4.at[part, mine], r4).start()

            return carry

        lax.fori_loop(0, 16, one, 0)

    def wait_all(buf, sem):
        pltpu.make_async_copy(buf, buf, sem).wait()

    def gathered(lr, b):
        wanted = recv1[lr, b * 32 : b * 32 + 32].astype(F32).reshape(256, 128).astype(BF)
        blocks = dot(perms[1], wanted, 1, 0).astype(BF)
        return [blocks[k * 64 : k * 64 + 64] for k in range(4)]

    def messages(rows_of):
        stack = jnp.concatenate(rows_of, axis=0)
        return dot(perms[2], stack, 1, 0).reshape(32, 8, 128).astype(BF)

    def multiply_outgoing():
        wait_all(recv1.at[1], r1.at[1])
        for b in range(4):
            for k, block in enumerate(gathered(1, b)):
                right[core, b * 64 : b * 64 + 64, k * 128 : k * 128 + 128] = block
        relay = pltpu.make_async_remote_copy(
            src_ref=right.at[core], dst_ref=right.at[core], send_sem=sx, recv_sem=rx, device_id=sibling,
            device_id_type=MESH,
        )
        relay.start()
        wait_all(recv1.at[0], r1.at[0])
        for b in range(4):
            for k, block in enumerate(gathered(0, b)):
                left[b * 64 : b * 64 + 64, k * 128 : k * 128 + 128] = block
        relay.wait_recv()
        top = (number >> 6) & 1
        for flip in (1, 0):
            first = pl.multiple_of((top ^ flip) * 128, 128)
            rows = left[pl.ds(first, 128), :]
            halves = [dot(rows, right[j], 1, 1).astype(BF) for j in range(2)]
            for b in range(2):
                send2[pl.ds((top ^ flip) * 64 + b * 32, 32)] = messages(
                    [halves[j // 2][b * 64 : b * 64 + 64, (j % 2) * 128 : (j % 2) * 128 + 128] for j in range(4)]
                )
            scatter_products([m for m in XY_MASKS if m[1] >> 1 == flip])
        return relay

    def multiply_incoming():
        wait_all(recv3, r3)
        for b in range(8):
            wanted = recv3[b * 16 : b * 16 + 16].reshape(256, 128)
            blocks = dot(perms[5], wanted, 1, 0).astype(BF)
            for lr in range(2):
                for k in range(4):
                    pairs[lr, b * 32 : b * 32 + 32, k * 128 : k * 128 + 128] = blocks[
                        lr * 128 + k * 32 : lr * 128 + k * 32 + 32
                    ]
        top = (number >> 6) & 1
        for flip in (1, 0):
            y1 = top ^ flip
            lhs = jnp.concatenate(
                [pairs[0, :, pl.ds(pl.multiple_of(zl * 256 + y1 * 128, 128), 128)] for zl in range(2)], axis=1
            )
            part = dot(lhs, pairs[1], 0, 0).astype(BF)
            for b in range(4):
                send4[pl.ds((b // 2) * 128 + y1 * 64 + (b % 2) * 32, 32)] = messages(
                    [part[b * 64 : b * 64 + 64, j * 128 : j * 128 + 128] for j in range(4)]
                )
            scatter_parts([m for m in XY_MASKS if m[1] >> 1 == flip])

    def by_channel(buf, b):
        block = buf[b * 32 : b * 32 + 32].astype(F32).reshape(256, 128).astype(BF)
        return dot(perms[3], block, 1, 0)

    def finish(u, source, target):
        if u == 0:
            wait_all(recv2, r2)
        else:
            wait_all(recv4, r4)
        for b in range(4):
            if u == 0:
                tiles = by_channel(recv2, b)
            else:
                tiles = by_channel(recv4.at[0], b) + by_channel(recv4.at[1], b)
            for j in range(8):
                chan[b * 32 : b * 32 + 32, j * 128 : j * 128 + 128] = tiles[j * 32 : j * 32 + 32]
        gain = gains_ref[u, 1:2, :].reshape(128, 1)
        for p in range(4):
            row, half = p // 2, p % 2
            lanes = slice(half * 256, half * 256 + 256)
            values = chan[:, p * 256 : p * 256 + 256]
            centred = values - jnp.mean(values, axis=0, keepdims=True)
            variance = jnp.mean(centred * centred, axis=0, keepdims=True)
            scaled = (centred * lax.rsqrt(variance + 1e-05) * gain).astype(BF)
            projected = dot(scaled, wo_ref[u], 0, 0)
            gating = jax.nn.sigmoid(dot(normed[u, row, lanes, :], wg_ref[u], 1, 0))
            updated = source[row, lanes, :].astype(F32) + gating * projected
            target[row, lanes, :] = updated.astype(BF)

    normalize_rows(0, z_ref)
    for lr in (1, 0):
        edge_map(0, lr)
        pack_one(lr)
    pl.semaphore_wait(barrier, 128)
    scatter_edges(1)
    scatter_edges(0)
    relay = multiply_outgoing()
    finish(0, z_ref, cur)

    normalize_rows(1, cur)
    edges_of(pl.multiple_of(zlo * 64, 64))
    scatter_pairs(False)
    edges_of(pl.multiple_of((1 - zlo) * 64, 64))
    scatter_pairs(True)
    multiply_incoming()
    finish(1, cur, out_ref)

    relay.wait_send()
    wait_all(send3.at[pl.ds(0, 127)], s3)
    wait_all(send4.at[pl.ds(0, 255)], s4)

    @pl.when(zlo == core)
    def _():
        for lr in range(2):
            wait_all(send1.at[lr, pl.ds(0, 127)], s1.at[lr])
        wait_all(send2.at[pl.ds(0, 127)], s2)

    @pl.when(zlo != core)
    def _():
        for lr in range(2):
            wait_all(send1.at[lr], s1.at[lr])
        wait_all(send2, s2)


def per_device(pair_map, pair_mask, edge_weights, gate_weights, out_weights, norm_gains):
    return pl.pallas_call(
        kernel,
        out_shape=jax.ShapeDtypeStruct((2, 512, 128), BF),
        in_specs=[pl.BlockSpec(memory_space=pl.ANY)] * 6,
        out_specs=pl.BlockSpec(memory_space=pltpu.VMEM),
        scratch_shapes=[
            pltpu.VMEM((2, 512, 128), BF),
            pltpu.VMEM((2, 512), jnp.int32),
            pltpu.VMEM((2, 128, 512), BF),
            pltpu.VMEM((2, 128, 128), BF),
            pltpu.VMEM((2, 128, 128), BF),
            pltpu.VMEM((2, 2, 128), F32),
            pltpu.VMEM((2, 512, 128), BF),
            pltpu.VMEM((6, 256, 256), BF),
            pltpu.VMEM((2, 2, 512, 128), BF),
            pltpu.VMEM((2, 512, 128), BF),
            pltpu.VMEM((2, 128, 1024), BF),
            pltpu.VMEM((2, 128, 8, 128), BF),
            pltpu.VMEM((2, 128, 8, 128), BF),
            pltpu.VMEM((256, 512), BF),
            pltpu.VMEM((2, 256, 512), BF),
            pltpu.VMEM((128, 8, 128), BF),
            pltpu.VMEM((128, 8, 128), BF),
            pltpu.VMEM((128, 16, 128), BF),
            pltpu.VMEM((128, 16, 128), BF),
            pltpu.VMEM((2, 256, 512), BF),
            pltpu.VMEM((256, 8, 128), BF),
            pltpu.VMEM((2, 128, 8, 128), BF),
            pltpu.VMEM((128, 1024), F32),
            pltpu.SemaphoreType.DMA((2,)),
            pltpu.SemaphoreType.DMA((2,)),
        ]
        + [pltpu.SemaphoreType.DMA] * 8
        + [
            pltpu.SemaphoreType.DMA((6,)),
        ],
        compiler_params=pltpu.CompilerParams(
            collective_id=0, has_side_effects=True, vmem_limit_bytes=40 * 1024 * 1024
        ),
        name="triangles",
    )(pair_map, pair_mask, edge_weights, gate_weights, out_weights, norm_gains)


def solution(mesh):
    return jax.shard_map(
        per_device,
        mesh=mesh,
        in_specs=(P(("dap", "grp"), None, None), P(("dap", "grp"), None), P(), P(), P(), P()),
        out_specs=P(("dap", "grp"), None, None),
        check_vma=False,
    )
```

```python
import functools

import jax
import jax.numpy as jnp
from jax import lax
from jax.experimental import pallas as pl
from jax.experimental.pallas import tpu as pltpu
from jax.sharding import PartitionSpec as P

BF = jnp.bfloat16
F32 = jnp.float32
MESH = pl.DeviceIdType.MESH


def dot(a, b, ca, cb):
    return lax.dot_general(a, b, (((ca,), (cb,)), ((), ())), preferred_element_type=F32)


def one_hot(source):
    rows = lax.broadcasted_iota(jnp.int32, (256, 256), 0)
    cols = lax.broadcasted_iota(jnp.int32, (256, 256), 1)
    return jnp.where(cols == source(rows), 1.0, 0.0).astype(BF)


def ring(mask):
    return (0, 1, 2, 1)[mask]


XY_MASKS = sorted(((x, y) for x in range(4) for y in range(4)), key=lambda m: -ring(m[0]) - ring(m[1]))
Z_MASKS = (4, 5, 7, 3, 2, 6, 1, 0)
Z_EVEN = (4, 2, 6, 0)
Z_ODD = (5, 7, 3, 1)


def packed(masks):
    return sum((((m & 1) << 3) | (m >> 1)) << (4 * i) for i, m in enumerate(masks) if i < 7)


def nibble(word, i):
    return (word >> (4 * i)) & 15


def mesh_id(number):
    return (number >> 2, number & 3)


def kernel(z_hbm, mask_hbm, we_hbm, wg_hbm, wo_hbm, gains_hbm, out_ref,
           z_ref, mask_ref, we_ref, wg_ref, wo_ref, gains_ref, wt, perms, normed, cur, edges, send1, recv1, left, right, send2, recv2,
           send3, recv3, pairs, send4, recv4, chan, s1, r1, s2, r2, s3, r3, s4, r4, sx, rx, load):
    dap = lax.axis_index("dap")
    number = dap * 4 + lax.axis_index("grp")
    core = (number >> 2) & 1
    zlo = number >> 7
    slot = number & 127
    channel = ((number >> 3) << 2) | (number & 3)
    sibling = mesh_id(number ^ 4)

    loads = [
        pltpu.make_async_copy(src, dst, load.at[i])
        for i, (src, dst) in enumerate(
            ((z_hbm, z_ref), (we_hbm, we_ref), (gains_hbm, gains_ref), (mask_hbm, mask_ref),
             (wg_hbm, wg_ref), (wo_hbm, wo_ref))
        )
    ]
    for copy in loads:
        copy.start()

    barrier = pltpu.get_barrier_semaphore()

    def partners(visit, masks=XY_MASKS):
        word = jnp.where(zlo == core, packed(Z_EVEN), packed(Z_ODD))
        chip = number - core * 4

        def one(k, carry):
            z = nibble(word, k & 3)
            base = chip ^ (((z >> 3) << 7) | (z & 3) | ((k >> 2) << 2))
            for mx, my in masks:
                visit(base ^ (my << 5 | mx << 3), mx == 0 and my == 0)
            return carry

        lax.fori_loop(0, 8, one, 0)

    def greet(other, maybe_here):
        def signal():
            pl.semaphore_signal(barrier, inc=1, device_id=mesh_id(other), device_id_type=MESH)

        if maybe_here:
            pl.when((other | 4) != (number | 4))(signal)
        else:
            signal()

    pl.semaphore_signal(barrier, inc=1, device_id=sibling, device_id_type=MESH)
    partners(greet)

    perms[0] = one_hot(lambda r: (r % 8) * 32 + r // 8)
    perms[1] = one_hot(lambda r: ((r // 2) % 32) * 8 + (r % 2) * 4 + r // 64)
    perms[4] = one_hot(lambda r: (r % 16) * 16 + r // 16)
    perms[5] = one_hot(lambda r: ((r // 2) % 16) * 16 + (r // 128) * 8 + (r % 2) * 4 + (r // 32) % 4)
    perms[2] = one_hot(lambda r: (r % 4) * 64 + r // 4)
    perms[3] = one_hot(lambda r: (r % 32) * 8 + r // 32)

    for copy in loads:
        copy.wait()
    for u in range(2):
        wt[u] = we_ref[u].astype(F32).T.astype(BF)

    def normalize_rows(u, source):
        gain = gains_ref[u, 0:1, :]
        for p in range(4):
            row, lanes = p // 2, slice(p % 2 * 256, p % 2 * 256 + 256)
            zf = source[row, lanes, :].astype(F32)
            centred = zf - jnp.mean(zf, axis=1, keepdims=True)
            variance = jnp.mean(centred * centred, axis=1, keepdims=True)
            normed[u, row, lanes, :] = (centred * lax.rsqrt(variance + 1e-05) * gain).astype(BF)

    def edge_map(u, lr):
        for p in range(4):
            row, lanes = p // 2, slice(p % 2 * 256, p % 2 * 256 + 256)
            mask = mask_ref[row : row + 1, lanes].astype(F32)
            proj = dot(wt[u, lr * 256 : lr * 256 + 256, :], normed[u, row, lanes, :], 1, 1)
            edge = jax.nn.sigmoid(proj[:128]) * proj[128:] * mask
            edges[lr, :, p * 256 : p * 256 + 256] = edge.astype(BF)

    def pack_one(lr):
        for b in range(4):
            rows = slice(b * 32, b * 32 + 32)
            stack = jnp.concatenate([edges[lr, rows, j * 128 : j * 128 + 128] for j in range(8)], axis=0)
            send1[lr, rows] = dot(perms[0], stack, 1, 0).reshape(32, 8, 128).astype(BF)

    def edges_of(base):
        weights = jnp.concatenate([wt[1, pl.ds(base + c * 128, 64), :] for c in range(4)], axis=0)
        for p in range(4):
            row, lanes = p // 2, slice(p % 2 * 256, p % 2 * 256 + 256)
            mask = mask_ref[row : row + 1, lanes].astype(F32)
            proj = dot(weights, normed[1, row, lanes, :], 1, 1)
            for lr in range(2):
                gate, value = proj[lr * 128 : lr * 128 + 64], proj[lr * 128 + 64 : lr * 128 + 128]
                edges[lr, 0:64, p * 256 : p * 256 + 256] = (jax.nn.sigmoid(gate) * value * mask).astype(BF)
        for b in range(4):
            rows = slice(b * 16, b * 16 + 16)
            stack = jnp.concatenate(
                [edges[lr, rows, j * 128 : j * 128 + 128] for lr in range(2) for j in range(8)], axis=0
            )
            send3[pl.ds(base + b * 16, 16)] = dot(perms[4], stack, 1, 0).astype(BF).reshape(16, 16, 128)

    def scatter_edges(lr):
        base = (number - core * 4) | (zlo << 2)

        def one(k, carry):
            z = jnp.where(k == 7, 0, nibble(packed(Z_MASKS), k))
            for mx, my in XY_MASKS:
                other = base ^ (((z >> 3) << 7) | (z & 3) | (my << 5 | mx << 3))
                h = channel ^ (((z >> 3) << 6) | (z & 3) | (my << 4 | mx << 2))
                copy = pltpu.make_async_remote_copy(
                    src_ref=send1.at[lr, h], dst_ref=recv1.at[lr, slot], send_sem=s1.at[lr],
                    recv_sem=r1.at[lr],
                    device_id=mesh_id(other), device_id_type=MESH,
                )
                if mx or my:
                    copy.start()
                    continue
                pl.when(other != number)(copy.start)

                @pl.when(other == number)
                def _():
                    pltpu.make_async_copy(send1.at[lr, h], recv1.at[lr, slot], r1.at[lr]).start()

            return carry

        lax.fori_loop(0, 8, one, 0)

    def scatter_products(masks):
        def send(other, maybe_self):
            at = other & 127
            copy = pltpu.make_async_remote_copy(
                src_ref=send2.at[at], dst_ref=recv2.at[channel], send_sem=s2, recv_sem=r2,
                device_id=mesh_id(other), device_id_type=MESH,
            )
            if not maybe_self:
                copy.start()
                return
            pl.when(other != number)(copy.start)

            @pl.when(other == number)
            def _():
                pltpu.make_async_copy(send2.at[at], recv2.at[channel], r2).start()

        partners(send, masks)

    mine = ((number >> 2) << 1) | (number & 1)

    def scatter_pairs(odd):
        z = ((number & 3) << 1) | zlo
        plane = number & (15 << 3)

        def one(k, carry):
            worker_core = k & 1
            step = k >> 1
            dz = jnp.where(step == 0, 1, 7) if odd else jnp.where(step == 0, 2 + 4 * worker_core, 0)
            wz = (z + dz) & 7
            base = ((wz & 1) << 7) | plane | (worker_core << 2) | (wz >> 1)
            for mx, my in XY_MASKS:
                other = base ^ (my << 5 | mx << 3)
                h = ((other >> 2) << 1) | (other & 1)
                copy = pltpu.make_async_remote_copy(
                    src_ref=send3.at[h], dst_ref=recv3.at[mine], send_sem=s3, recv_sem=r3,
                    device_id=mesh_id(other), device_id_type=MESH,
                )
                if mx or my:
                    copy.start()
                    continue
                pl.when(other != number)(copy.start)

                @pl.when(other == number)
                def _():
                    pltpu.make_async_copy(send3.at[h], recv3.at[mine], r3).start()

            return carry

        lax.fori_loop(0, 4, one, 0)

    def scatter_parts(masks):
        part = (number >> 1) & 1

        def one(k, carry):
            zk = k >> 1
            z = jnp.where(zk == 7, 0, nibble(packed(Z_MASKS), zk))
            base = number ^ (((z >> 3) << 7) | (z & 3) | ((k & 1) << 2))
            for mx, my in masks:
                other = base ^ (my << 5 | mx << 3)
                copy = pltpu.make_async_remote_copy(
                    src_ref=send4.at[other], dst_ref=recv4.at[part, mine], send_sem=s4, recv_sem=r4,
                    device_id=mesh_id(other), device_id_type=MESH,
                )
                if mx or my:
                    copy.start()
                    continue
                pl.when(other != number)(copy.start)

                @pl.when(other == number)
                def _():
                    pltpu.make_async_copy(send4.at[other], recv4.at[part, mine], r4).start()

            return carry

        lax.fori_loop(0, 16, one, 0)

    def wait_all(buf, sem):
        pltpu.make_async_copy(buf, buf, sem).wait()

    def gathered(lr, b):
        wanted = recv1[lr, pl.ds(b * 32, 32)].astype(F32).reshape(256, 128).astype(BF)
        blocks = dot(perms[1], wanted, 1, 0).astype(BF)
        return [blocks[k * 64 : k * 64 + 64] for k in range(4)]

    def messages(rows_of):
        stack = jnp.concatenate(rows_of, axis=0)
        return dot(perms[2], stack, 1, 0).reshape(32, 8, 128).astype(BF)

    def multiply_outgoing():
        wait_all(recv1.at[1], r1.at[1])
        for b in range(4):
            for k, block in enumerate(gathered(1, b)):
                right[core, b * 64 : b * 64 + 64, k * 128 : k * 128 + 128] = block
        relay = pltpu.make_async_remote_copy(
            src_ref=right.at[core], dst_ref=right.at[core], send_sem=sx, recv_sem=rx, device_id=sibling,
            device_id_type=MESH,
        )
        relay.start()
        wait_all(recv1.at[0], r1.at[0])
        top = (number >> 6) & 1
        for flip in (1, 0):
            for b in range(2):
                for k, block in enumerate(gathered(0, (top ^ flip) * 2 + b)):
                    left[flip, b * 64 : b * 64 + 64, k * 128 : k * 128 + 128] = block
            rows = left[flip]
            if flip:
                relay.wait_recv()
            halves = [dot(rows, right[j], 1, 1).astype(BF) for j in range(2)]
            for b in range(2):
                send2[pl.ds((top ^ flip) * 64 + b * 32, 32)] = messages(
                    [halves[j // 2][b * 64 : b * 64 + 64, (j % 2) * 128 : (j % 2) * 128 + 128] for j in range(4)]
                )
            scatter_products([m for m in XY_MASKS if m[1] >> 1 == flip])
        return relay

    def multiply_incoming():
        wait_all(recv3, r3)
        for b in range(8):
            wanted = recv3[b * 16 : b * 16 + 16].reshape(256, 128)
            blocks = dot(perms[5], wanted, 1, 0).astype(BF)
            for lr in range(2):
                for k in range(4):
                    pairs[lr, b * 32 : b * 32 + 32, k * 128 : k * 128 + 128] = blocks[
                        lr * 128 + k * 32 : lr * 128 + k * 32 + 32
                    ]
        top = (number >> 6) & 1
        for flip in (1, 0):
            y1 = top ^ flip
            lhs = jnp.concatenate(
                [pairs[0, :, pl.ds(pl.multiple_of(zl * 256 + y1 * 128, 128), 128)] for zl in range(2)], axis=1
            )
            part = dot(lhs, pairs[1], 0, 0).astype(BF)
            for b in range(4):
                send4[pl.ds((b // 2) * 128 + y1 * 64 + (b % 2) * 32, 32)] = messages(
                    [part[b * 64 : b * 64 + 64, j * 128 : j * 128 + 128] for j in range(4)]
                )
            scatter_parts([m for m in XY_MASKS if m[1] >> 1 == flip])

    def by_channel(buf, b):
        block = buf[b * 32 : b * 32 + 32].astype(F32).reshape(256, 128).astype(BF)
        return dot(perms[3], block, 1, 0)

    def finish(u, source, target):
        if u == 0:
            wait_all(recv2, r2)
        else:
            wait_all(recv4, r4)
        for b in range(4):
            if u == 0:
                tiles = by_channel(recv2, b)
            else:
                tiles = by_channel(recv4.at[0], b) + by_channel(recv4.at[1], b)
            for j in range(8):
                chan[b * 32 : b * 32 + 32, j * 128 : j * 128 + 128] = tiles[j * 32 : j * 32 + 32]
        gain = gains_ref[u, 1:2, :].reshape(128, 1)
        for p in range(4):
            row, half = p // 2, p % 2
            lanes = slice(half * 256, half * 256 + 256)
            values = chan[:, p * 256 : p * 256 + 256]
            centred = values - jnp.mean(values, axis=0, keepdims=True)
            variance = jnp.mean(centred * centred, axis=0, keepdims=True)
            scaled = (centred * lax.rsqrt(variance + 1e-05) * gain).astype(BF)
            projected = dot(scaled, wo_ref[u], 0, 0)
            gating = jax.nn.sigmoid(dot(normed[u, row, lanes, :], wg_ref[u], 1, 0))
            updated = source[row, lanes, :].astype(F32) + gating * projected
            target[row, lanes, :] = updated.astype(BF)

    normalize_rows(0, z_ref)
    for lr in (1, 0):
        edge_map(0, lr)
        pack_one(lr)
    pl.semaphore_wait(barrier, 128)
    scatter_edges(1)
    scatter_edges(0)
    relay = multiply_outgoing()
    finish(0, z_ref, cur)

    normalize_rows(1, cur)
    edges_of(pl.multiple_of(zlo * 64, 64))
    scatter_pairs(False)
    edges_of(pl.multiple_of((1 - zlo) * 64, 64))
    scatter_pairs(True)
    multiply_incoming()
    finish(1, cur, out_ref)

    relay.wait_send()
    wait_all(send3.at[pl.ds(0, 127)], s3)
    wait_all(send4.at[pl.ds(0, 255)], s4)

    @pl.when(zlo == core)
    def _():
        for lr in range(2):
            wait_all(send1.at[lr, pl.ds(0, 127)], s1.at[lr])
        wait_all(send2.at[pl.ds(0, 127)], s2)

    @pl.when(zlo != core)
    def _():
        for lr in range(2):
            wait_all(send1.at[lr], s1.at[lr])
        wait_all(send2, s2)


def per_device(pair_map, pair_mask, edge_weights, gate_weights, out_weights, norm_gains):
    return pl.pallas_call(
        kernel,
        out_shape=jax.ShapeDtypeStruct((2, 512, 128), BF),
        in_specs=[pl.BlockSpec(memory_space=pl.ANY)] * 6,
        out_specs=pl.BlockSpec(memory_space=pltpu.VMEM),
        scratch_shapes=[
            pltpu.VMEM((2, 512, 128), BF),
            pltpu.VMEM((2, 512), jnp.int32),
            pltpu.VMEM((2, 128, 512), BF),
            pltpu.VMEM((2, 128, 128), BF),
            pltpu.VMEM((2, 128, 128), BF),
            pltpu.VMEM((2, 2, 128), F32),
            pltpu.VMEM((2, 512, 128), BF),
            pltpu.VMEM((6, 256, 256), BF),
            pltpu.VMEM((2, 2, 512, 128), BF),
            pltpu.VMEM((2, 512, 128), BF),
            pltpu.VMEM((2, 128, 1024), BF),
            pltpu.VMEM((2, 128, 8, 128), BF),
            pltpu.VMEM((2, 128, 8, 128), BF),
            pltpu.VMEM((2, 128, 512), BF),
            pltpu.VMEM((2, 256, 512), BF),
            pltpu.VMEM((128, 8, 128), BF),
            pltpu.VMEM((128, 8, 128), BF),
            pltpu.VMEM((128, 16, 128), BF),
            pltpu.VMEM((128, 16, 128), BF),
            pltpu.VMEM((2, 256, 512), BF),
            pltpu.VMEM((256, 8, 128), BF),
            pltpu.VMEM((2, 128, 8, 128), BF),
            pltpu.VMEM((128, 1024), F32),
            pltpu.SemaphoreType.DMA((2,)),
            pltpu.SemaphoreType.DMA((2,)),
        ]
        + [pltpu.SemaphoreType.DMA] * 8
        + [
            pltpu.SemaphoreType.DMA((6,)),
        ],
        compiler_params=pltpu.CompilerParams(
            collective_id=0, has_side_effects=True, vmem_limit_bytes=40 * 1024 * 1024
        ),
        name="triangles",
    )(pair_map, pair_mask, edge_weights, gate_weights, out_weights, norm_gains)


def solution(mesh):
    return jax.shard_map(
        per_device,
        mesh=mesh,
        in_specs=(P(("dap", "grp"), None, None), P(("dap", "grp"), None), P(), P(), P(), P()),
        out_specs=P(("dap", "grp"), None, None),
        check_vma=False,
    )
```

```python
import functools

import jax
import jax.numpy as jnp
from jax import lax
from jax.experimental import pallas as pl
from jax.experimental.pallas import tpu as pltpu
from jax.sharding import PartitionSpec as P

BF = jnp.bfloat16
F32 = jnp.float32
MESH = pl.DeviceIdType.MESH


def dot(a, b, ca, cb):
    return lax.dot_general(a, b, (((ca,), (cb,)), ((), ())), preferred_element_type=F32)


def one_hot(source):
    rows = lax.broadcasted_iota(jnp.int32, (256, 256), 0)
    cols = lax.broadcasted_iota(jnp.int32, (256, 256), 1)
    return jnp.where(cols == source(rows), 1.0, 0.0).astype(BF)


def ring(mask):
    return (0, 1, 2, 1)[mask]


XY_MASKS = sorted(((x, y) for x in range(4) for y in range(4)), key=lambda m: -ring(m[0]) - ring(m[1]))
Z_MASKS = (4, 5, 7, 3, 2, 6, 1, 0)
Z_EVEN = (4, 2, 6, 0)
Z_ODD = (5, 7, 3, 1)


def packed(masks):
    return sum((((m & 1) << 3) | (m >> 1)) << (4 * i) for i, m in enumerate(masks) if i < 7)


def nibble(word, i):
    return (word >> (4 * i)) & 15


def mesh_id(number):
    return (number >> 2, number & 3)


def kernel(z_hbm, mask_hbm, we_hbm, wg_hbm, wo_hbm, gains_hbm, out_ref,
           z_ref, mask_ref, we_ref, wg_ref, wo_ref, gains_ref, wt, perms, normed, cur, edges, send1, recv1, left, right, send2, recv2,
           send3, recv3, pairs, send4, recv4, chan, s1, r1, s2, r2, s3, r3, s4, r4, sx, rx, load):
    dap = lax.axis_index("dap")
    number = dap * 4 + lax.axis_index("grp")
    core = (number >> 2) & 1
    zlo = number >> 7
    slot = number & 127
    channel = ((number >> 3) << 2) | (number & 3)
    sibling = mesh_id(number ^ 4)

    loads = [
        pltpu.make_async_copy(src, dst, load.at[i])
        for i, (src, dst) in enumerate(
            ((z_hbm, z_ref), (we_hbm, we_ref), (gains_hbm, gains_ref), (mask_hbm, mask_ref),
             (wg_hbm, wg_ref), (wo_hbm, wo_ref))
        )
    ]
    for copy in loads:
        copy.start()

    barrier = pltpu.get_barrier_semaphore()

    def partners(visit, masks=XY_MASKS):
        word = jnp.where(zlo == core, packed(Z_EVEN), packed(Z_ODD))
        chip = number - core * 4

        def one(k, carry):
            z = nibble(word, k >> 1)
            base = chip ^ (((z >> 3) << 7) | (z & 3) | ((k & 1) << 2))
            for mx, my in masks:
                visit(base ^ (my << 5 | mx << 3), mx == 0 and my == 0)
            return carry

        lax.fori_loop(0, 8, one, 0)

    def greet(other, maybe_here):
        def signal():
            pl.semaphore_signal(barrier, inc=1, device_id=mesh_id(other), device_id_type=MESH)

        if maybe_here:
            pl.when((other | 4) != (number | 4))(signal)
        else:
            signal()

    pl.semaphore_signal(barrier, inc=1, device_id=sibling, device_id_type=MESH)
    partners(greet)

    perms[0] = one_hot(lambda r: (r % 8) * 32 + r // 8)
    perms[1] = one_hot(lambda r: ((r // 2) % 32) * 8 + (r % 2) * 4 + r // 64)
    perms[4] = one_hot(lambda r: (r % 16) * 16 + r // 16)
    perms[5] = one_hot(lambda r: ((r // 2) % 16) * 16 + (r // 128) * 8 + (r % 2) * 4 + (r // 32) % 4)
    perms[2] = one_hot(lambda r: (r % 4) * 64 + r // 4)
    perms[3] = one_hot(lambda r: (r % 32) * 8 + r // 32)

    for copy in loads:
        copy.wait()
    for u in range(2):
        wt[u] = we_ref[u].astype(F32).T.astype(BF)

    def normalize_rows(u, source):
        gain = gains_ref[u, 0:1, :]
        for p in range(4):
            row, lanes = p // 2, slice(p % 2 * 256, p % 2 * 256 + 256)
            zf = source[row, lanes, :].astype(F32)
            centred = zf - jnp.mean(zf, axis=1, keepdims=True)
            variance = jnp.mean(centred * centred, axis=1, keepdims=True)
            normed[u, row, lanes, :] = (centred * lax.rsqrt(variance + 1e-05) * gain).astype(BF)

    def edge_map(u, lr):
        for p in range(4):
            row, lanes = p // 2, slice(p % 2 * 256, p % 2 * 256 + 256)
            mask = mask_ref[row : row + 1, lanes].astype(F32)
            proj = dot(wt[u, lr * 256 : lr * 256 + 256, :], normed[u, row, lanes, :], 1, 1)
            edge = jax.nn.sigmoid(proj[:128]) * proj[128:] * mask
            edges[lr, :, p * 256 : p * 256 + 256] = edge.astype(BF)

    def pack_one(lr):
        for b in range(4):
            rows = slice(b * 32, b * 32 + 32)
            stack = jnp.concatenate([edges[lr, rows, j * 128 : j * 128 + 128] for j in range(8)], axis=0)
            send1[lr, rows] = dot(perms[0], stack, 1, 0).reshape(32, 8, 128).astype(BF)

    def edges_of(base):
        weights = jnp.concatenate([wt[1, pl.ds(base + c * 128, 64), :] for c in range(4)], axis=0)
        for p in range(4):
            row, lanes = p // 2, slice(p % 2 * 256, p % 2 * 256 + 256)
            mask = mask_ref[row : row + 1, lanes].astype(F32)
            proj = dot(weights, normed[1, row, lanes, :], 1, 1)
            for lr in range(2):
                gate, value = proj[lr * 128 : lr * 128 + 64], proj[lr * 128 + 64 : lr * 128 + 128]
                edges[lr, 0:64, p * 256 : p * 256 + 256] = (jax.nn.sigmoid(gate) * value * mask).astype(BF)
        for b in range(4):
            rows = slice(b * 16, b * 16 + 16)
            stack = jnp.concatenate(
                [edges[lr, rows, j * 128 : j * 128 + 128] for lr in range(2) for j in range(8)], axis=0
            )
            send3[pl.ds(base + b * 16, 16)] = dot(perms[4], stack, 1, 0).astype(BF).reshape(16, 16, 128)

    def scatter_edges(lr):
        base = (number - core * 4) | (zlo << 2)

        def one(k, carry):
            z = jnp.where(k == 7, 0, nibble(packed(Z_MASKS), k))
            for mx, my in XY_MASKS:
                other = base ^ (((z >> 3) << 7) | (z & 3) | (my << 5 | mx << 3))
                h = channel ^ (((z >> 3) << 6) | (z & 3) | (my << 4 | mx << 2))
                copy = pltpu.make_async_remote_copy(
                    src_ref=send1.at[lr, h], dst_ref=recv1.at[lr, slot], send_sem=s1.at[lr],
                    recv_sem=r1.at[lr],
                    device_id=mesh_id(other), device_id_type=MESH,
                )
                if mx or my:
                    copy.start()
                    continue
                pl.when(other != number)(copy.start)

                @pl.when(other == number)
                def _():
                    pltpu.make_async_copy(send1.at[lr, h], recv1.at[lr, slot], r1.at[lr]).start()

            return carry

        lax.fori_loop(0, 8, one, 0)

    def scatter_products(masks):
        def send(other, maybe_self):
            at = other & 127
            copy = pltpu.make_async_remote_copy(
                src_ref=send2.at[at], dst_ref=recv2.at[channel], send_sem=s2, recv_sem=r2,
                device_id=mesh_id(other), device_id_type=MESH,
            )
            if not maybe_self:
                copy.start()
                return
            pl.when(other != number)(copy.start)

            @pl.when(other == number)
            def _():
                pltpu.make_async_copy(send2.at[at], recv2.at[channel], r2).start()

        partners(send, masks)

    mine = ((number >> 2) << 1) | (number & 1)

    def scatter_pairs(odd):
        z = ((number & 3) << 1) | zlo
        plane = number & (15 << 3)

        def one(k, carry):
            worker_core = k & 1
            step = k >> 1
            dz = jnp.where(step == 0, 1, 7) if odd else jnp.where(step == 0, 2 + 4 * worker_core, 0)
            wz = (z + dz) & 7
            base = ((wz & 1) << 7) | plane | (worker_core << 2) | (wz >> 1)
            for mx, my in XY_MASKS:
                other = base ^ (my << 5 | mx << 3)
                h = ((other >> 2) << 1) | (other & 1)
                copy = pltpu.make_async_remote_copy(
                    src_ref=send3.at[h], dst_ref=recv3.at[mine], send_sem=s3, recv_sem=r3,
                    device_id=mesh_id(other), device_id_type=MESH,
                )
                if mx or my:
                    copy.start()
                    continue
                pl.when(other != number)(copy.start)

                @pl.when(other == number)
                def _():
                    pltpu.make_async_copy(send3.at[h], recv3.at[mine], r3).start()

            return carry

        lax.fori_loop(0, 4, one, 0)

    def scatter_parts(masks):
        part = (number >> 1) & 1

        def one(k, carry):
            zk = k >> 1
            z = jnp.where(zk == 7, 0, nibble(packed(Z_MASKS), zk))
            base = number ^ (((z >> 3) << 7) | (z & 3) | ((k & 1) << 2))
            for mx, my in masks:
                other = base ^ (my << 5 | mx << 3)
                copy = pltpu.make_async_remote_copy(
                    src_ref=send4.at[other], dst_ref=recv4.at[part, mine], send_sem=s4, recv_sem=r4,
                    device_id=mesh_id(other), device_id_type=MESH,
                )
                if mx or my:
                    copy.start()
                    continue
                pl.when(other != number)(copy.start)

                @pl.when(other == number)
                def _():
                    pltpu.make_async_copy(send4.at[other], recv4.at[part, mine], r4).start()

            return carry

        lax.fori_loop(0, 16, one, 0)

    def wait_all(buf, sem):
        pltpu.make_async_copy(buf, buf, sem).wait()

    def gathered(lr, b):
        wanted = recv1[lr, pl.ds(b * 32, 32)].astype(F32).reshape(256, 128).astype(BF)
        blocks = dot(perms[1], wanted, 1, 0).astype(BF)
        return [blocks[k * 64 : k * 64 + 64] for k in range(4)]

    def messages(rows_of):
        stack = jnp.concatenate(rows_of, axis=0)
        return dot(perms[2], stack, 1, 0).reshape(32, 8, 128).astype(BF)

    def multiply_outgoing():
        wait_all(recv1.at[1], r1.at[1])
        for b in range(4):
            for k, block in enumerate(gathered(1, b)):
                right[core, b * 64 : b * 64 + 64, k * 128 : k * 128 + 128] = block
        relay = pltpu.make_async_remote_copy(
            src_ref=right.at[core], dst_ref=right.at[core], send_sem=sx, recv_sem=rx, device_id=sibling,
            device_id_type=MESH,
        )
        relay.start()
        wait_all(recv1.at[0], r1.at[0])
        top = (number >> 6) & 1
        for flip in (1, 0):
            for b in range(2):
                for k, block in enumerate(gathered(0, (top ^ flip) * 2 + b)):
                    left[flip, b * 64 : b * 64 + 64, k * 128 : k * 128 + 128] = block
            rows = left[flip]
            if flip:
                relay.wait_recv()
            halves = [dot(rows, right[j], 1, 1).astype(BF) for j in range(2)]
            for b in range(2):
                send2[pl.ds((top ^ flip) * 64 + b * 32, 32)] = messages(
                    [halves[j // 2][b * 64 : b * 64 + 64, (j % 2) * 128 : (j % 2) * 128 + 128] for j in range(4)]
                )
            scatter_products([m for m in XY_MASKS if m[1] >> 1 == flip])
        return relay

    def multiply_incoming():
        wait_all(recv3, r3)
        for b in range(8):
            wanted = recv3[b * 16 : b * 16 + 16].reshape(256, 128)
            blocks = dot(perms[5], wanted, 1, 0).astype(BF)
            for lr in range(2):
                for k in range(4):
                    pairs[lr, b * 32 : b * 32 + 32, k * 128 : k * 128 + 128] = blocks[
                        lr * 128 + k * 32 : lr * 128 + k * 32 + 32
                    ]
        top = (number >> 6) & 1
        for flip in (1, 0):
            y1 = top ^ flip
            lhs = jnp.concatenate(
                [pairs[0, :, pl.ds(pl.multiple_of(zl * 256 + y1 * 128, 128), 128)] for zl in range(2)], axis=1
            )
            part = dot(lhs, pairs[1], 0, 0).astype(BF)
            for b in range(4):
                send4[pl.ds((b // 2) * 128 + y1 * 64 + (b % 2) * 32, 32)] = messages(
                    [part[b * 64 : b * 64 + 64, j * 128 : j * 128 + 128] for j in range(4)]
                )
            scatter_parts([m for m in XY_MASKS if m[1] >> 1 == flip])

    def by_channel(buf, b):
        block = buf[b * 32 : b * 32 + 32].astype(F32).reshape(256, 128).astype(BF)
        return dot(perms[3], block, 1, 0)

    def finish(u, source, target):
        if u == 0:
            wait_all(recv2, r2)
        else:
            wait_all(recv4, r4)
        for b in range(4):
            if u == 0:
                tiles = by_channel(recv2, b)
            else:
                tiles = by_channel(recv4.at[0], b) + by_channel(recv4.at[1], b)
            for j in range(8):
                chan[b * 32 : b * 32 + 32, j * 128 : j * 128 + 128] = tiles[j * 32 : j * 32 + 32]
        gain = gains_ref[u, 1:2, :].reshape(128, 1)
        for p in range(4):
            row, half = p // 2, p % 2
            lanes = slice(half * 256, half * 256 + 256)
            values = chan[:, p * 256 : p * 256 + 256]
            centred = values - jnp.mean(values, axis=0, keepdims=True)
            variance = jnp.mean(centred * centred, axis=0, keepdims=True)
            scaled = (centred * lax.rsqrt(variance + 1e-05) * gain).astype(BF)
            projected = dot(scaled, wo_ref[u], 0, 0)
            gating = jax.nn.sigmoid(dot(normed[u, row, lanes, :], wg_ref[u], 1, 0))
            updated = source[row, lanes, :].astype(F32) + gating * projected
            target[row, lanes, :] = updated.astype(BF)

    normalize_rows(0, z_ref)
    for lr in (1, 0):
        edge_map(0, lr)
        pack_one(lr)
    pl.semaphore_wait(barrier, 128)
    scatter_edges(1)
    scatter_edges(0)
    relay = multiply_outgoing()
    finish(0, z_ref, cur)

    normalize_rows(1, cur)
    edges_of(pl.multiple_of(zlo * 64, 64))
    scatter_pairs(False)
    edges_of(pl.multiple_of((1 - zlo) * 64, 64))
    scatter_pairs(True)
    multiply_incoming()
    finish(1, cur, out_ref)

    relay.wait_send()
    wait_all(send3.at[pl.ds(0, 127)], s3)
    wait_all(send4.at[pl.ds(0, 255)], s4)

    @pl.when(zlo == core)
    def _():
        for lr in range(2):
            wait_all(send1.at[lr, pl.ds(0, 127)], s1.at[lr])
        wait_all(send2.at[pl.ds(0, 127)], s2)

    @pl.when(zlo != core)
    def _():
        for lr in range(2):
            wait_all(send1.at[lr], s1.at[lr])
        wait_all(send2, s2)


def per_device(pair_map, pair_mask, edge_weights, gate_weights, out_weights, norm_gains):
    return pl.pallas_call(
        kernel,
        out_shape=jax.ShapeDtypeStruct((2, 512, 128), BF),
        in_specs=[pl.BlockSpec(memory_space=pl.ANY)] * 6,
        out_specs=pl.BlockSpec(memory_space=pltpu.VMEM),
        scratch_shapes=[
            pltpu.VMEM((2, 512, 128), BF),
            pltpu.VMEM((2, 512), jnp.int32),
            pltpu.VMEM((2, 128, 512), BF),
            pltpu.VMEM((2, 128, 128), BF),
            pltpu.VMEM((2, 128, 128), BF),
            pltpu.VMEM((2, 2, 128), F32),
            pltpu.VMEM((2, 512, 128), BF),
            pltpu.VMEM((6, 256, 256), BF),
            pltpu.VMEM((2, 2, 512, 128), BF),
            pltpu.VMEM((2, 512, 128), BF),
            pltpu.VMEM((2, 128, 1024), BF),
            pltpu.VMEM((2, 128, 8, 128), BF),
            pltpu.VMEM((2, 128, 8, 128), BF),
            pltpu.VMEM((2, 128, 512), BF),
            pltpu.VMEM((2, 256, 512), BF),
            pltpu.VMEM((128, 8, 128), BF),
            pltpu.VMEM((128, 8, 128), BF),
            pltpu.VMEM((128, 16, 128), BF),
            pltpu.VMEM((128, 16, 128), BF),
            pltpu.VMEM((2, 256, 512), BF),
            pltpu.VMEM((256, 8, 128), BF),
            pltpu.VMEM((2, 128, 8, 128), BF),
            pltpu.VMEM((128, 1024), F32),
            pltpu.SemaphoreType.DMA((2,)),
            pltpu.SemaphoreType.DMA((2,)),
        ]
        + [pltpu.SemaphoreType.DMA] * 8
        + [
            pltpu.SemaphoreType.DMA((6,)),
        ],
        compiler_params=pltpu.CompilerParams(
            collective_id=0, has_side_effects=True, vmem_limit_bytes=40 * 1024 * 1024
        ),
        name="triangles",
    )(pair_map, pair_mask, edge_weights, gate_weights, out_weights, norm_gains)


def solution(mesh):
    return jax.shard_map(
        per_device,
        mesh=mesh,
        in_specs=(P(("dap", "grp"), None, None), P(("dap", "grp"), None), P(), P(), P(), P()),
        out_specs=P(("dap", "grp"), None, None),
        check_vma=False,
    )
```
